32 devices in a mesh: elem: 32 (over z, y, x, core).
Axes of the slice: x: 2, y: 2, z: 4, core: 2. Of those that a mesh axis runs over, the one named last changes fastest.
Arguments:
- elem_mats: bfloat16 [384, 750, 750], P('elem'), may hold values from -0.14 to 0.64
- face_blocks: bfloat16 [864, 125, 125], P('elem'), may hold values from -0.45 to 1.25
- rhs: bfloat16 [864, 16, 125], P('elem'), may hold values from -6 to 6
- elem_faces: int32 [384, 6], replicated, may hold values from 0 to 863, as said below
- orient: int32 [384, 6], replicated, may hold values from 0 to 7
- counts: int32 [32], replicated, may hold values from 3 to 9, as said below
Outputs:
- traces: float32 [864, 16, 125], P('elem')
The draws below stay inside these ranges and needn't reach their ends.
Inputs may be any that keep to these rules, and one draw needn't show every extreme that they name: Element slots 0 to counts[d] - 1 of device d (rows d * 12 onward) are live, the others empty; counts[2 i] + counts[2 i + 1] = 12. `elem_faces`: face f is owned by device f // 27. A live element slot of device d has all its faces owned by devices d - 2 to d + 2; device d has exactly 4 live element faces owned by each other device within that distance; a face is listed by at most two live element faces. Rows of empty slots hold arbitrary faces.
All inputs are finite; a program needn't handle non-finite values.
Results may differ from the reference program's by a relative error of at most 0.0017.
Values may be sent and summed in bfloat16 or wider, within the bound.
No kernel may reach another device: no remote copies, remote signals or barrier semaphores. Data moves between devices by JAX's collectives and lax.ppermute only.
A program may use at most 128 MiB of HBM per device.

```python
import math
import jax
import jax.numpy as jnp
import numpy as np
from jax import lax

COMP = 5
EDGE = 5
NFUN = 16
E_CAP = 12
ITERS = 2
REACH = 2
TRACE = 125
DOF = 750
SLOT = 4
FACE_DEV = 27
NELEM = 384
FACES = 864
N_ELEM = 32


def build_layout(key):
    lowest = E_CAP // 4
    pair_total = N_ELEM // 2
    per_device = 6 * E_CAP
    total_slots = N_ELEM * per_device
    heavier = jax.random.randint(jax.random.fold_in(key, 101), (pair_total,), E_CAP // 2, E_CAP - lowest + 1)
    extreme = jax.random.randint(jax.random.fold_in(key, 102), (), 0, pair_total)
    heavier = jnp.where(jnp.arange(pair_total) == extreme, E_CAP - lowest, heavier)
    flipped = jax.random.randint(jax.random.fold_in(key, 103), (pair_total,), 0, 2)
    even_count = jnp.where(flipped == 0, heavier, E_CAP - heavier)
    counts = jnp.stack([even_count, E_CAP - even_count], axis=1).reshape(N_ELEM).astype(jnp.int32)
    device_of = jnp.arange(total_slots, dtype=jnp.int32) // per_device
    slot_of = jnp.arange(total_slots, dtype=jnp.int32) % per_device
    is_live = slot_of // 6 < counts[device_of]
    scores = jax.random.randint(jax.random.fold_in(key, 104), (total_slots,), 0, 1 << 20) * per_device + slot_of
    scores = jnp.where(is_live, scores, scores + (1 << 30))
    order_in = jnp.argsort(scores.reshape(N_ELEM, per_device), axis=1)
    rank_in = jnp.argsort(order_in, axis=1).reshape(total_slots).astype(jnp.int32)
    offsets = jnp.array(list(range(1, REACH + 1)) + [-step_size for step_size in range(1, REACH + 1)], jnp.int32)
    bucket = rank_in // SLOT
    offset_of = offsets[jnp.clip(bucket, 0, 2 * REACH - 1)]
    target = device_of + offset_of
    sending = is_live & (bucket < 2 * REACH) & (target >= 0) & (target < N_ELEM)
    target = jnp.where(sending, target, device_of)
    group_of = jnp.where(is_live, target, N_ELEM)
    shuffled = jax.random.permutation(jax.random.fold_in(key, 105), total_slots)
    sorted_pos = shuffled[jnp.argsort(group_of[shuffled], stable=True)]
    group_sizes = jnp.zeros((N_ELEM + 1,), jnp.int32).at[group_of].add(1)
    starts = jnp.cumsum(group_sizes) - group_sizes
    position = jnp.arange(total_slots, dtype=jnp.int32) - starts[group_of[sorted_pos]]
    place_in = jnp.zeros((total_slots,), jnp.int32).at[sorted_pos].set(position)
    face_ids = jnp.where(is_live, target * FACE_DEV + place_in // 2, device_of * FACE_DEV)
    return (counts, face_ids.reshape(N_ELEM * E_CAP, 6).astype(jnp.int32))


def draw_counts(key, part):
    return build_layout(key)[0]


def draw_elem_faces(key, part):
    return build_layout(key)[1]


def draw_elem_mats(key, part):
    shape = (N_ELEM * E_CAP, DOF, DOF)
    noise = jax.random.truncated_normal(key, -6.0, 6.0, shape, jnp.float32)
    return (0.5 * jnp.eye(DOF, dtype=jnp.float32) + 0.15 / math.sqrt(DOF) * noise).astype(jnp.bfloat16)


def draw_face_blocks(key, part):
    shape = (FACE_DEV * N_ELEM, TRACE, TRACE)
    noise = jax.random.truncated_normal(key, -6.0, 6.0, shape, jnp.float32)
    return (0.8 * jnp.eye(TRACE, dtype=jnp.float32) + 0.2 / math.sqrt(TRACE) * noise).astype(jnp.bfloat16)


def place_ends(entries, key, smallest, high):
    longest = entries.shape.index(max(entries.shape))
    spots = []
    for shift in (0, 1):
        where = [jax.random.randint(jax.random.fold_in(key, axis), (), 0, length) for axis, length in enumerate(entries.shape)]
        where[longest] = (where[longest] + shift) % entries.shape[longest]
        spots.append(tuple(where))
    return entries.at[spots[0]].set(smallest).at[spots[1]].set(high)


def block_levels(key, dims, shards, least, largest):
    level, own = 1.0, jax.random.fold_in(key, 6)
    for axis_at, parts in shards:
        draws = jnp.exp(jax.random.uniform(jax.random.fold_in(own, axis_at), (parts,), jnp.float32, least / len(shards), largest / len(shards)))
        level = level * jnp.repeat(draws, dims[axis_at] // parts).reshape([-1 if axis == axis_at else 1 for axis in range(len(dims))])
    return level


def gaussian(key, dims, spread, reach, split=(), kind=jnp.bfloat16):
    gain = block_levels(key, dims, split, -0.22, 0.18) if split else 1.0
    values = jax.random.normal(key, dims, jnp.float32) * spread * gain
    return jnp.minimum(jnp.maximum(values, -reach), reach).astype(kind)


def setup_inputs(seed: int = 0) -> dict:
    arg_keys = jax.random.split(jax.random.key(seed), 7)
    elem_mats = draw_elem_mats(jax.random.fold_in(arg_keys[6], 71), 0)
    face_blocks = draw_face_blocks(jax.random.fold_in(arg_keys[6], 71), 0)
    rhs = gaussian(arg_keys[2], (FACES, NFUN, TRACE), 1.0, 6.0, ((0, 32),))
    elem_faces = draw_elem_faces(jax.random.fold_in(arg_keys[6], 71), 0)
    orient = place_ends(jax.random.randint(arg_keys[4], (NELEM, 6), 0, 8), jax.random.fold_in(arg_keys[4], 1), 0, 7).astype(jnp.int32)
    counts = draw_counts(jax.random.fold_in(arg_keys[6], 71), 0)
    return dict(elem_mats=elem_mats, face_blocks=face_blocks, rhs=rhs, elem_faces=elem_faces, orient=orient, counts=counts)


def orient_tables(edge_nodes, components):
    node_ids = np.arange(edge_nodes * edge_nodes)
    row_pos = node_ids // edge_nodes
    col_pos = node_ids % edge_nodes
    table_rows = []
    for orient_code in range(8):
        if orient_code & 4:
            first_pos, second_pos = col_pos, row_pos
        else:
            first_pos, second_pos = row_pos, col_pos
        if orient_code & 1:
            first_pos = edge_nodes - 1 - first_pos
        if orient_code & 2:
            second_pos = edge_nodes - 1 - second_pos
        moved_node = first_pos * edge_nodes + second_pos
        table_rows.append(np.concatenate([part_index * edge_nodes * edge_nodes + moved_node for part_index in range(components)]))
    forward = np.stack(table_rows).astype(np.int32)
    backward = np.argsort(forward, axis=1).astype(np.int32)
    return forward, backward


def per_device(operands):
    traces_block, matrix_block = operands
    return jnp.einsum("akni,akilj->alnj", traces_block.astype(jnp.float32), matrix_block.astype(jnp.float32))


def reference(elem_mats, face_blocks, rhs, elem_faces, orient, counts):
    forward, backward = orient_tables(EDGE, COMP)
    to_element = jnp.asarray(forward)[orient]
    to_face = jnp.asarray(backward)[orient]
    slot_pos = jnp.arange(N_ELEM * E_CAP, dtype=jnp.int32)
    live_rows = (slot_pos % E_CAP) < counts[slot_pos // E_CAP]
    face_count = face_blocks.shape[0]
    matrices = elem_mats.reshape(N_ELEM, E_CAP, 6, TRACE, 6, TRACE)
    traces = jnp.zeros(rhs.shape, jnp.float32)
    for sweep_index in range(ITERS):
        rounded = traces.astype(jnp.bfloat16)
        gathered = rounded[elem_faces]
        elem_frame = jnp.take_along_axis(gathered, to_element[:, :, None, :], axis=3)
        elem_terms = lax.map(per_device, (elem_frame.reshape(N_ELEM, E_CAP, 6, NFUN, TRACE), matrices))
        elem_terms = elem_terms.reshape(N_ELEM * E_CAP, 6, NFUN, TRACE)
        elem_terms = jnp.where(live_rows[:, None, None, None], elem_terms, jnp.zeros_like(elem_terms)).astype(jnp.bfloat16)
        face_terms = jnp.take_along_axis(elem_terms, to_face[:, :, None, :], axis=3)
        summed = jax.ops.segment_sum(face_terms.reshape(N_ELEM * E_CAP * 6, NFUN, TRACE).astype(jnp.float32), elem_faces.reshape(-1), num_segments=face_count)
        residual = (rhs.astype(jnp.float32) - summed).astype(jnp.bfloat16)
        traces = traces + jnp.einsum("fni,fij->fnj", residual.astype(jnp.float32), face_blocks.astype(jnp.float32))
    return traces
```

```python
import functools

import jax
import jax.numpy as jnp
import numpy as np
from jax import lax
from jax.experimental import pallas as pl
from jax.experimental.pallas import tpu as pltpu
from jax.sharding import PartitionSpec as P

COMP = 5
EDGE = 5
SLOT = 4
LANES = 128
SIB, CROSS, EVEN, ODD = range(4)


def orient_tables(edge_nodes, components):
    node_ids = np.arange(edge_nodes * edge_nodes)
    row_pos = node_ids // edge_nodes
    col_pos = node_ids % edge_nodes
    table_rows = []
    for orient_code in range(8):
        if orient_code & 4:
            first_pos, second_pos = (col_pos, row_pos)
        else:
            first_pos, second_pos = (row_pos, col_pos)
        if orient_code & 1:
            first_pos = edge_nodes - 1 - first_pos
        if orient_code & 2:
            second_pos = edge_nodes - 1 - second_pos
        moved_node = first_pos * edge_nodes + second_pos
        table_rows.append(
            np.concatenate(
                [
                    part_index * edge_nodes * edge_nodes + moved_node
                    for part_index in range(components)
                ]
            )
        )
    forward = np.stack(table_rows).astype(np.int32)
    backward = np.argsort(forward, axis=1).astype(np.int32)
    return (forward, backward)


def lane_tables(trace_len):
    forward, backward = orient_tables(EDGE, COMP)
    gap = LANES - trace_len
    spare = np.arange(trace_len, LANES)
    lanes = np.arange(LANES)
    into = np.zeros((6 * 8, LANES), np.int32)
    outof = np.zeros((6 * 8, LANES), np.int32)
    for k in range(6):
        for code in range(8):
            full = np.concatenate([forward[code], spare])
            into[k * 8 + code] = full[(lanes + gap * k) % LANES]
            full = np.concatenate([backward[code], spare])
            outof[k * 8 + code] = (full - gap * k) % LANES
    return into, outof


def swap_routes(devices):
    routes = [[(i, i ^ 1) for i in range(devices)]]
    for shift in (0, 2):
        route = []
        for i in range(devices):
            other = ((i - shift) ^ 2) + shift
            route.append((i, other if 0 <= i - shift and 0 <= other < devices else i ^ 1))
        routes.append(route)
    return routes


def partners(me):
    core = me & 1
    odd_chip = (me >> 1) & 1
    return (
        me ^ 1,
        me - 1 + 2 * core,
        me + 2 - 4 * odd_chip,
        me - 2 + 4 * odd_chip,
    )


def first_kernel(
    elem_cap, devices, faces, counts, rhs, blocks, traces, rounded, swap, even, odd, slots, found
):
    me = lax.axis_index("elem")
    face_dev, functionals, trace_len = rhs.shape
    for f in range(face_dev):
        value = jnp.dot(rhs[f], blocks[f], preferred_element_type=jnp.float32)
        traces[f] = jnp.zeros((functionals, LANES), jnp.float32)
        traces[f, :, :trace_len] = value
        rounded[f] = traces[f].astype(jnp.bfloat16)
    for group, device in enumerate(partners(me)):
        valid = (device >= 0) & (device < devices)
        safe = jnp.clip(device, 0, devices - 1)
        live = jnp.where(valid, counts[safe], 0)
        for r in range(SLOT):
            found[group * 8 + r] = 0

        def scan(e, rank):
            for k in range(6):
                local = faces[k, safe * elem_cap + e] - me * face_dev
                hit = (local >= 0) & (local < face_dev)
                found[group * 8 + rank] = local
                rank = rank + hit.astype(jnp.int32)
            return rank

        lax.fori_loop(0, live, scan, jnp.int32(0))
        for r in range(SLOT):
            slot = jnp.where(valid, found[group * 8 + r], 0)
            slots[group * SLOT + r] = jnp.where(valid, slot, face_dev)
            tile = rounded[slot]
            if group < 2:
                swap[group * SLOT + r] = tile
            elif group == EVEN:
                even[r] = tile
            else:
                odd[r] = tile


def second_kernel(
    elem_cap,
    faces,
    orient,
    counts,
    rounded,
    from_sib,
    from_even,
    from_odd,
    into,
    outof,
    mats,
    home,
    swap,
    even,
    odd,
    table,
    acc,
    rows,
    heads,
):
    me = lax.axis_index("elem")
    face_dev, functionals, _ = rounded.shape
    live = elem_cap - elem_cap // 4
    trace_len = mats.shape[1] // 6
    gap = LANES - trace_len
    spare = face_dev + 4 * SLOT
    core = me & 1
    odd_chip = (me >> 1) & 1

    table[:face_dev] = rounded[...]
    table[face_dev : face_dev + SLOT] = from_sib[:SLOT]
    crossing = jnp.broadcast_to((core ^ odd_chip) == 1, (SLOT, functionals, LANES))
    table[face_dev + SLOT : face_dev + 2 * SLOT] = jnp.where(
        crossing, from_even[SLOT:], from_odd[SLOT:]
    )
    table[face_dev + 2 * SLOT : face_dev + 3 * SLOT] = from_even[:SLOT]
    table[face_dev + 3 * SLOT : face_dev + 4 * SLOT] = from_odd[:SLOT]
    table[spare] = jnp.zeros((functionals, LANES), jnp.bfloat16)
    acc[...] = jnp.zeros_like(acc)

    heads[0] = face_dev + SLOT * jnp.where(odd_chip == 1, EVEN, ODD)
    heads[1] = face_dev + SLOT * jnp.where(core == 1, SIB, CROSS)
    heads[3] = face_dev + SLOT * jnp.where(core == 1, CROSS, SIB)
    heads[4] = face_dev + SLOT * jnp.where(odd_chip == 1, ODD, EVEN)
    count = counts[me]
    magic = (1 << 16) // face_dev + 1
    places = []
    codes = []
    for e in range(live):
        for k in range(6):
            rel = faces[k, me * elem_cap + e] - (me - 2) * face_dev
            used = e < count
            rel = jnp.where(used, rel, 2 * face_dev)
            owner = (rel * magic) >> 16
            head = heads[owner]
            heads[owner] = head + 1
            place = jnp.where(owner == 2, rel - 2 * face_dev, head)
            places.append(jnp.where(used, place, spare))
            codes.append(orient[k, me * elem_cap + e])

    lane = lax.broadcasted_iota(jnp.int32, (functionals, LANES), 1)
    for e in range(live):
        parts = []
        for k in range(6):
            tile = table[places[6 * e + k]].astype(jnp.float32)
            index = jnp.broadcast_to(
                into[pl.ds(k * 8 + codes[6 * e + k], 1), :], (functionals, LANES)
            )
            parts.append(jnp.take_along_axis(tile, index, axis=1, mode="promise_in_bounds"))
        for k in range(6):
            later = parts[k + 1] if k < 5 else jnp.zeros_like(parts[k])
            merged = jnp.where(lane < trace_len - gap * k, parts[k], later)
            rows[e, :, k * LANES : (k + 1) * LANES] = merged.astype(jnp.bfloat16)
    for e in range(live):
        terms = jnp.dot(
            rows[e, :, : 6 * trace_len], mats[e], preferred_element_type=jnp.float32
        )
        terms = jnp.concatenate(
            [terms, jnp.zeros((functionals, 6 * gap), jnp.float32)], axis=1
        ).astype(jnp.bfloat16).astype(jnp.float32)
        for k in range(6):
            tile = terms[:, k * LANES : (k + 1) * LANES]
            if k:
                before = terms[:, (k - 1) * LANES : k * LANES]
                tile = jnp.where(lane >= LANES - gap * k, before, tile)
            index = jnp.broadcast_to(
                outof[pl.ds(k * 8 + codes[6 * e + k], 1), :], (functionals, LANES)
            )
            tile = jnp.take_along_axis(tile, index, axis=1, mode="promise_in_bounds")
            place = places[6 * e + k]
            acc[place] = acc[place] + tile
    home[...] = acc[:face_dev]
    swap[...] = acc[face_dev : face_dev + 2 * SLOT].astype(jnp.bfloat16)
    even[...] = acc[face_dev + 2 * SLOT : face_dev + 3 * SLOT].astype(jnp.bfloat16)
    odd[...] = acc[face_dev + 3 * SLOT : face_dev + 4 * SLOT].astype(jnp.bfloat16)


def third_kernel(slots, home, from_sib, from_even, from_odd, rhs, blocks, traces, out, acc):
    me = lax.axis_index("elem")
    face_dev, functionals, trace_len = rhs.shape
    core = me & 1
    odd_chip = (me >> 1) & 1
    acc[:face_dev] = home[...]
    crossing = jnp.broadcast_to((core ^ odd_chip) == 1, (functionals, LANES))
    for r in range(SLOT):
        arrived = [
            from_sib[r],
            jnp.where(crossing, from_even[SLOT + r], from_odd[SLOT + r]),
            from_even[r],
            from_odd[r],
        ]
        for group in range(4):
            place = slots[group * SLOT + r]
            acc[place] = acc[place] + arrived[group].astype(jnp.float32)
    for f in range(face_dev):
        residual = rhs[f].astype(jnp.float32) - acc[f, :, :trace_len]
        update = jnp.dot(
            residual.astype(jnp.bfloat16), blocks[f], preferred_element_type=jnp.float32
        )
        out[f] = traces[f, :, :trace_len] + update


def exchange(routes, swap, even, odd):
    sibling, even_chips, odd_chips = routes
    got = lax.ppermute(swap, "elem", sibling)
    relay = got[SLOT:]
    from_even = lax.ppermute(jnp.concatenate([even, relay]), "elem", even_chips)
    from_odd = lax.ppermute(jnp.concatenate([odd, relay]), "elem", odd_chips)
    return got, from_even, from_odd


def per_device(devices, elem_mats, face_blocks, rhs, elem_faces, orient, counts):
    elem_cap, dof, _ = elem_mats.shape
    face_dev, functionals, trace_len = rhs.shape
    live = elem_cap - elem_cap // 4
    routes = swap_routes(devices)
    faces = elem_faces.T
    codes = orient.T
    into, outof = lane_tables(trace_len)
    vmem = pl.BlockSpec(memory_space=pltpu.VMEM)
    smem = pl.BlockSpec(memory_space=pltpu.SMEM)

    def tiles(count, kind):
        return jax.ShapeDtypeStruct((count, functionals, LANES), kind)

    params = pltpu.CompilerParams(vmem_limit_bytes=48 << 20)
    traces, rounded, swap, even, odd, slots = pl.pallas_call(
        functools.partial(first_kernel, elem_cap, devices),
        out_shape=(
            tiles(face_dev, jnp.float32),
            tiles(face_dev, jnp.bfloat16),
            tiles(2 * SLOT, jnp.bfloat16),
            tiles(SLOT, jnp.bfloat16),
            tiles(SLOT, jnp.bfloat16),
            jax.ShapeDtypeStruct((4 * SLOT,), jnp.int32),
        ),
        in_specs=[smem, smem, vmem, vmem],
        out_specs=(vmem, vmem, vmem, vmem, vmem, smem),
        scratch_shapes=[pltpu.SMEM((32,), jnp.int32)],
        compiler_params=params,
        name="first_sweep",
    )(faces, counts, rhs, face_blocks)
    from_sib, from_even, from_odd = exchange(routes, swap, even, odd)
    home, swap, even, odd = pl.pallas_call(
        functools.partial(second_kernel, elem_cap),
        out_shape=(
            tiles(face_dev, jnp.float32),
            tiles(2 * SLOT, jnp.bfloat16),
            tiles(SLOT, jnp.bfloat16),
            tiles(SLOT, jnp.bfloat16),
        ),
        in_specs=[smem, smem, smem] + [vmem] * 7,
        out_specs=(vmem,) * 4,
        scratch_shapes=[
            pltpu.VMEM((face_dev + 4 * SLOT + 1, functionals, LANES), jnp.bfloat16),
            pltpu.VMEM((face_dev + 4 * SLOT + 1, functionals, LANES), jnp.float32),
            pltpu.VMEM((live, functionals, 6 * LANES), jnp.bfloat16),
            pltpu.SMEM((8,), jnp.int32),
        ],
        compiler_params=params,
        name="element_terms",
    )(
        faces,
        codes,
        counts,
        rounded,
        from_sib,
        from_even,
        from_odd,
        jnp.asarray(into),
        jnp.asarray(outof),
        elem_mats,
    )
    from_sib, from_even, from_odd = exchange(routes, swap, even, odd)
    return pl.pallas_call(
        third_kernel,
        out_shape=jax.ShapeDtypeStruct(rhs.shape, jnp.float32),
        in_specs=[smem] + [vmem] * 7,
        out_specs=vmem,
        scratch_shapes=[pltpu.VMEM((face_dev + 1, functionals, LANES), jnp.float32)],
        compiler_params=params,
        name="last_update",
    )(slots, home, from_sib, from_even, from_odd, rhs, face_blocks, traces)


def solution(mesh):
    in_specs = (P("elem", None, None), P("elem", None, None), P("elem", None, None), P(), P(), P())
    out_specs = P("elem", None, None)
    return jax.shard_map(
        functools.partial(per_device, mesh.shape["elem"]),
        mesh=mesh,
        in_specs=in_specs,
        out_specs=out_specs,
        check_vma=False,
    )
```

```python
import functools

import jax
import jax.numpy as jnp
import numpy as np
from jax import lax
from jax.experimental import pallas as pl
from jax.experimental.pallas import tpu as pltpu
from jax.sharding import PartitionSpec as P

COMP = 5
EDGE = 5
SLOT = 4
LANES = 128
SIB, EVEN, ODD, CROSS = range(4)


def orient_tables(edge_nodes, components):
    node_ids = np.arange(edge_nodes * edge_nodes)
    row_pos = node_ids // edge_nodes
    col_pos = node_ids % edge_nodes
    table_rows = []
    for orient_code in range(8):
        if orient_code & 4:
            first_pos, second_pos = (col_pos, row_pos)
        else:
            first_pos, second_pos = (row_pos, col_pos)
        if orient_code & 1:
            first_pos = edge_nodes - 1 - first_pos
        if orient_code & 2:
            second_pos = edge_nodes - 1 - second_pos
        moved_node = first_pos * edge_nodes + second_pos
        table_rows.append(
            np.concatenate(
                [
                    part_index * edge_nodes * edge_nodes + moved_node
                    for part_index in range(components)
                ]
            )
        )
    forward = np.stack(table_rows).astype(np.int32)
    backward = np.argsort(forward, axis=1).astype(np.int32)
    return (forward, backward)


def window_rows(trace_len):
    dof = 6 * trace_len
    for height in range(trace_len, dof):
        last = dof - height
        starts = [min(trace_len * k // 16 * 16, last) for k in range(6)]
        if last % 16 == 0 and all(
            start + height >= trace_len * (k + 1) for k, start in enumerate(starts)
        ):
            return height, last
    return dof, 0


def lane_tables(trace_len):
    forward, backward = orient_tables(EDGE, COMP)
    gap = LANES - trace_len
    spare = np.arange(trace_len, LANES)
    lanes = np.arange(LANES)
    _, last = window_rows(trace_len)
    into = np.zeros((6 * 8, LANES), np.int32)
    window = np.zeros((6 * 8, LANES), np.int32)
    outof = np.zeros((6 * 8, LANES), np.int32)
    for k in range(6):
        start = min(trace_len * k // 16 * 16, last)
        for code in range(8):
            full = np.concatenate([forward[code], spare])
            into[k * 8 + code] = full[(lanes + gap * k) % LANES]
            window[k * 8 + code] = full[(lanes - (trace_len * k - start)) % LANES]
            full = np.concatenate([backward[code], spare])
            outof[k * 8 + code] = (full - gap * k) % LANES
    return np.stack([into, window, outof])


def swap_routes(devices):
    routes = [[(i, i ^ 1) for i in range(devices)]]
    for shift in (0, 2):
        route = []
        for i in range(devices):
            other = ((i - shift) ^ 3) + shift
            route.append((i, other if i >= shift and other < devices else i ^ 1))
        routes.append(route)
    return routes


def partners(me):
    core = me & 1
    odd_chip = (me >> 1) & 1
    return (
        me ^ 1,
        me + 2 - 4 * odd_chip,
        me - 2 + 4 * odd_chip,
        me - 1 + 2 * core,
    )


def arrivals(me, from_sib, from_even, from_odd):
    shape = from_sib.shape[1:]
    by_even = jnp.broadcast_to(((me ^ (me >> 1)) & 1) == 1, shape)
    return [
        [from_sib[r] for r in range(SLOT)],
        [from_even[SLOT + r] for r in range(SLOT)],
        [from_odd[SLOT + r] for r in range(SLOT)],
        [jnp.where(by_even, from_even[r], from_odd[r]) for r in range(SLOT)],
    ]


def start_all(pairs, sems):
    copies = [
        pltpu.make_async_copy(src, dst, sems.at[i]) for i, (src, dst) in enumerate(pairs)
    ]
    for copy in copies:
        copy.start()
    return copies


def permuted(tile, index):
    index = jnp.broadcast_to(index, tile.shape)
    return jnp.take_along_axis(tile, index, axis=1, mode="promise_in_bounds")


def first_kernel(
    elem_cap,
    devices,
    faces_hbm,
    counts_hbm,
    rhs_hbm,
    blocks_hbm,
    traces,
    rounded,
    swap,
    cross,
    slots,
    faces,
    counts,
    rhs,
    blocks,
    found,
    sems,
):
    me = lax.axis_index("elem")
    face_dev, functionals, trace_len = rhs.shape
    copies = start_all(
        [(faces_hbm, faces), (counts_hbm, counts), (rhs_hbm, rhs), (blocks_hbm, blocks)], sems
    )
    copies[0].wait()
    copies[1].wait()
    for group, device in enumerate(partners(me)):
        valid = (device >= 0) & (device < devices)
        safe = jnp.clip(device, 0, devices - 1)
        live = jnp.where(valid, counts[safe], 0)
        for r in range(SLOT):
            found[group * 8 + r] = 0

        def scan(e, rank):
            for k in range(6):
                local = faces[k, safe * elem_cap + e] - me * face_dev
                hit = (local >= 0) & (local < face_dev)
                found[group * 8 + rank] = local
                rank = rank + hit.astype(jnp.int32)
            return rank

        lax.fori_loop(0, live, scan, jnp.int32(0))
        for r in range(SLOT):
            slots[group * SLOT + r] = jnp.where(valid, found[group * 8 + r], face_dev)
    copies[2].wait()
    copies[3].wait()
    for f in range(face_dev):
        value = jnp.dot(rhs[f], blocks[f], preferred_element_type=jnp.float32)
        traces[f] = jnp.zeros((functionals, LANES), jnp.float32)
        traces[f, :, :trace_len] = value
        rounded[f] = traces[f].astype(jnp.bfloat16)
    for group in range(4):
        for r in range(SLOT):
            slot = slots[group * SLOT + r]
            tile = rounded[jnp.where(slot < face_dev, slot, 0)]
            if group == CROSS:
                cross[r] = tile
            else:
                swap[group * SLOT + r] = tile


def home_kernel(
    elem_cap,
    faces_hbm,
    orient_hbm,
    counts_hbm,
    tables_hbm,
    rounded,
    mats,
    home,
    remote,
    index_in,
    index_out,
    terms,
    faces,
    orient,
    counts,
    tables,
    table,
    rows,
    heads,
    sems,
):
    me = lax.axis_index("elem")
    face_dev, functionals, _ = rounded.shape
    live = elem_cap - elem_cap // 4
    trace_len = mats.shape[1] // 6
    gap = LANES - trace_len
    far = 4 * SLOT
    copies = start_all(
        [(faces_hbm, faces), (orient_hbm, orient), (counts_hbm, counts), (tables_hbm, tables)], sems
    )
    table[:face_dev] = rounded[...]
    table[face_dev] = jnp.zeros((functionals, LANES), jnp.bfloat16)
    for copy in copies:
        copy.wait()
    groups = list(partners(me))
    for group, device in enumerate(groups):
        heads[device - me + 2] = group * SLOT
    heads[2] = 0
    index_in[...] = jnp.zeros_like(index_in)
    for t in range(far):
        remote[t] = live * 8
    count = counts[me]
    magic = (1 << 16) // face_dev + 1
    places = []
    picks = []
    for e in range(live):
        for k in range(6):
            rel = faces[k, me * elem_cap + e] - (me - 2) * face_dev
            used = e < count
            rel = jnp.where(used, rel, 2 * face_dev)
            owner = (rel * magic) >> 16
            head = heads[owner]
            heads[owner] = head + 1
            at_home = owner == 2
            place = jnp.where(at_home & used, rel - 2 * face_dev, face_dev)
            places.append(place)
            home[6 * e + k] = place
            slot = jnp.where(at_home, far, head)
            remote[slot] = e * 8 + k
            pick = k * 8 + orient[k, me * elem_cap + e]
            picks.append(pick)
            index_in[pl.ds(slot, 1), :] = tables[1, pl.ds(pick, 1), :]
            index_out[pl.ds(6 * e + k, 1), :] = tables[2, pl.ds(pick, 1), :]
    lane = lax.broadcasted_iota(jnp.int32, (functionals, LANES), 1)
    for e in range(live):
        parts = [
            permuted(
                table[places[6 * e + k]].astype(jnp.float32),
                tables[0, pl.ds(picks[6 * e + k], 1), :],
            )
            for k in range(6)
        ]
        for k in range(6):
            later = parts[k + 1] if k < 5 else jnp.zeros_like(parts[k])
            merged = jnp.where(lane < trace_len - gap * k, parts[k], later)
            rows[e, :, k * LANES : (k + 1) * LANES] = merged.astype(jnp.bfloat16)
    for e in range(live):
        terms[e, :, : 6 * trace_len] = jnp.dot(
            rows[e, :, : 6 * trace_len], mats[e], preferred_element_type=jnp.float32
        )


def remote_kernel(
    remote,
    index_in,
    index_out,
    from_sib,
    from_even,
    from_odd,
    before,
    mats,
    swap,
    cross,
    terms,
):
    me = lax.axis_index("elem")
    functionals = before.shape[1]
    live = before.shape[0]
    trace_len = mats.shape[1] // 6
    gap = LANES - trace_len
    height, last = window_rows(trace_len)
    terms[:live] = before[...]
    terms[live] = jnp.zeros(terms.shape[1:], jnp.float32)
    lane = lax.broadcasted_iota(jnp.int32, (functionals, LANES), 1)
    arrived = arrivals(me, from_sib, from_even, from_odd)
    where = []
    for group in range(4):
        for r in range(SLOT):
            t = group * SLOT + r
            packed = remote[t]
            e, k = packed >> 3, packed & 7
            where.append((e, k))
            start = jnp.minimum((trace_len * k) >> 4 << 4, last)
            shift = trace_len * k - start
            tile = permuted(arrived[group][r].astype(jnp.float32), index_in[t : t + 1, :])
            zero = jnp.zeros_like(tile)
            wide = jnp.concatenate(
                [
                    jnp.where((lane >= shift) & (lane < shift + trace_len), tile, zero),
                    jnp.where(lane < shift - gap, tile, zero),
                ],
                axis=1,
            ).astype(jnp.bfloat16)
            window = mats[jnp.minimum(e, live - 1), pl.ds(pl.multiple_of(start, 16), height), :]
            terms[e, :, : 6 * trace_len] += jnp.dot(
                wide[:, :height], window, preferred_element_type=jnp.float32
            )
    for group in range(4):
        for r in range(SLOT):
            t = group * SLOT + r
            e, k = where[t]
            tile = terms[e, :, pl.ds(pl.multiple_of(k * LANES, LANES), LANES)]
            ahead = jnp.maximum(k - 1, 0)
            left = terms[e, :, pl.ds(pl.multiple_of(ahead * LANES, LANES), LANES)]
            tile = jnp.where(lane >= LANES - gap * k, left, tile)
            pick = jnp.minimum(6 * e + k, 6 * live - 1)
            tile = permuted(tile, index_out[pl.ds(pick, 1), :]).astype(jnp.bfloat16)
            if group == CROSS:
                cross[r] = tile
            else:
                swap[group * SLOT + r] = tile


def scatter_kernel(home, index_out, terms, summed):
    functionals = summed.shape[1]
    live = terms.shape[0] - 1
    trace_len = COMP * EDGE * EDGE
    gap = LANES - trace_len
    lane = lax.broadcasted_iota(jnp.int32, (functionals, LANES), 1)
    summed[...] = jnp.zeros_like(summed)
    for e in range(live):
        for k in range(6):
            tile = terms[e, :, k * LANES : (k + 1) * LANES]
            if k:
                left = terms[e, :, (k - 1) * LANES : k * LANES]
                tile = jnp.where(lane >= LANES - gap * k, left, tile)
            i = 6 * e + k
            tile = permuted(tile, index_out[i : i + 1, :])
            place = home[i]
            summed[place] += tile.astype(jnp.bfloat16).astype(jnp.float32)


def last_kernel(slots, home, from_sib, from_even, from_odd, rhs, blocks, traces, out, summed):
    me = lax.axis_index("elem")
    face_dev, _, trace_len = rhs.shape
    summed[...] = home[...]
    arrived = arrivals(me, from_sib, from_even, from_odd)
    for group in range(4):
        for r in range(SLOT):
            place = slots[group * SLOT + r]
            summed[place] += arrived[group][r].astype(jnp.float32)
    for f in range(face_dev):
        residual = rhs[f].astype(jnp.float32) - summed[f, :, :trace_len]
        update = jnp.dot(
            residual.astype(jnp.bfloat16), blocks[f], preferred_element_type=jnp.float32
        )
        out[f] = traces[f, :, :trace_len] + update


def exchange(routes, swap, cross):
    sibling, even_chips, odd_chips = routes
    got = lax.ppermute(swap, "elem", sibling)
    even = jnp.concatenate([cross, got[SLOT : 2 * SLOT]])
    odd = jnp.concatenate([cross, got[2 * SLOT :]])
    return got, lax.ppermute(even, "elem", even_chips), lax.ppermute(odd, "elem", odd_chips)


def per_device(devices, elem_mats, face_blocks, rhs, elem_faces, orient, counts):
    elem_cap, dof, _ = elem_mats.shape
    face_dev, functionals, trace_len = rhs.shape
    live = elem_cap - elem_cap // 4
    far = 4 * SLOT
    routes = swap_routes(devices)

    def in_hbm(array):
        return pltpu.with_memory_space_constraint(array, pltpu.HBM)

    def in_vmem(array):
        return pltpu.with_memory_space_constraint(array, pltpu.VMEM)

    faces = in_hbm(elem_faces.T)
    codes = in_hbm(orient.T)
    counts = in_hbm(counts)
    tables = lane_tables(trace_len)
    vmem = pl.BlockSpec(memory_space=pltpu.VMEM)
    smem = pl.BlockSpec(memory_space=pltpu.SMEM)
    hbm = pl.BlockSpec(memory_space=pltpu.HBM)

    def tiles(count, kind, width=LANES):
        return jax.ShapeDtypeStruct((count, functionals, width), kind)

    def integers(*shape):
        return jax.ShapeDtypeStruct(shape, jnp.int32)

    params = pltpu.CompilerParams(vmem_limit_bytes=4 << 20)
    faces_smem = pltpu.SMEM(faces.shape, jnp.int32)
    counts_smem = pltpu.SMEM(counts.shape, jnp.int32)
    traces, rounded, swap, cross, slots = pl.pallas_call(
        functools.partial(first_kernel, elem_cap, devices),
        out_shape=(
            tiles(face_dev, jnp.float32),
            tiles(face_dev, jnp.bfloat16),
            tiles(3 * SLOT, jnp.bfloat16),
            tiles(SLOT, jnp.bfloat16),
            integers(far),
        ),
        in_specs=[hbm] * 4,
        out_specs=(vmem, vmem, vmem, vmem, smem),
        scratch_shapes=[
            faces_smem,
            counts_smem,
            pltpu.VMEM(rhs.shape, rhs.dtype),
            pltpu.VMEM(face_blocks.shape, face_blocks.dtype),
            pltpu.SMEM((32,), jnp.int32),
            pltpu.SemaphoreType.DMA((4,)),
        ],
        compiler_params=params,
        cost_estimate=pl.CostEstimate(
            flops=10**11, bytes_accessed=10**8, transcendentals=0
        ),
        name="first_sweep",
    )(faces, counts, in_hbm(rhs), in_hbm(face_blocks))
    from_sib, from_even, from_odd = exchange(routes, swap, cross)
    home, remote, index_in, index_out, terms = pl.pallas_call(
        functools.partial(home_kernel, elem_cap),
        out_shape=(
            integers(6 * live),
            integers(far + 1),
            integers(far + 1, LANES),
            integers(6 * live, LANES),
            tiles(live, jnp.float32, 6 * LANES),
        ),
        in_specs=[hbm] * 4 + [vmem] * 2,
        out_specs=(smem, smem, vmem, vmem, vmem),
        scratch_shapes=[
            faces_smem,
            faces_smem,
            counts_smem,
            pltpu.VMEM(tables.shape, jnp.int32),
            pltpu.VMEM((face_dev + 1, functionals, LANES), jnp.bfloat16),
            pltpu.VMEM((live, functionals, 6 * LANES), jnp.bfloat16),
            pltpu.SMEM((8,), jnp.int32),
            pltpu.SemaphoreType.DMA((4,)),
        ],
        compiler_params=params,
        cost_estimate=pl.CostEstimate(
            flops=2 * live * functionals * dof * dof,
            bytes_accessed=2 * live * dof * dof,
            transcendentals=0,
        ),
        name="home_terms",
    )(faces, codes, counts, in_hbm(jnp.asarray(tables)), rounded, in_vmem(elem_mats))
    swap, cross, terms = pl.pallas_call(
        remote_kernel,
        out_shape=(
            tiles(3 * SLOT, jnp.bfloat16),
            tiles(SLOT, jnp.bfloat16),
            tiles(live + 1, jnp.float32, 6 * LANES),
        ),
        in_specs=[smem] + [vmem] * 7,
        out_specs=(vmem,) * 3,
        compiler_params=params,
        name="remote_terms",
    )(remote, index_in, index_out, from_sib, from_even, from_odd, terms, in_vmem(elem_mats))
    from_sib, from_even, from_odd = exchange(routes, swap, cross)
    summed = pl.pallas_call(
        scatter_kernel,
        out_shape=tiles(face_dev + 1, jnp.float32),
        in_specs=[smem] + [vmem] * 2,
        out_specs=vmem,
        compiler_params=params,
        name="home_sum",
    )(home, index_out, terms)
    return pl.pallas_call(
        last_kernel,
        out_shape=jax.ShapeDtypeStruct(rhs.shape, jnp.float32),
        in_specs=[smem] + [vmem] * 7,
        out_specs=vmem,
        scratch_shapes=[pltpu.VMEM((face_dev + 1, functionals, LANES), jnp.float32)],
        compiler_params=params,
        name="last_update",
    )(slots, summed, from_sib, from_even, from_odd, rhs, face_blocks, traces)


def solution(mesh):
    in_specs = (P("elem", None, None), P("elem", None, None), P("elem", None, None), P(), P(), P())
    out_specs = P("elem", None, None)
    return jax.shard_map(
        functools.partial(per_device, mesh.shape["elem"]),
        mesh=mesh,
        in_specs=in_specs,
        out_specs=out_specs,
        check_vma=False,
    )
```

```python
import functools

import jax
import jax.numpy as jnp
import numpy as np
from jax import lax
from jax.experimental import pallas as pl
from jax.experimental.pallas import tpu as pltpu
from jax.sharding import PartitionSpec as P

COMP = 5
EDGE = 5
SLOT = 4
LANES = 128
SIB, EVEN, ODD, CROSS = range(4)


def orient_tables(edge_nodes, components):
    node_ids = np.arange(edge_nodes * edge_nodes)
    row_pos = node_ids // edge_nodes
    col_pos = node_ids % edge_nodes
    table_rows = []
    for orient_code in range(8):
        if orient_code & 4:
            first_pos, second_pos = (col_pos, row_pos)
        else:
            first_pos, second_pos = (row_pos, col_pos)
        if orient_code & 1:
            first_pos = edge_nodes - 1 - first_pos
        if orient_code & 2:
            second_pos = edge_nodes - 1 - second_pos
        moved_node = first_pos * edge_nodes + second_pos
        table_rows.append(
            np.concatenate(
                [
                    part_index * edge_nodes * edge_nodes + moved_node
                    for part_index in range(components)
                ]
            )
        )
    forward = np.stack(table_rows).astype(np.int32)
    backward = np.argsort(forward, axis=1).astype(np.int32)
    return (forward, backward)


def window_rows(trace_len):
    dof = 6 * trace_len
    for height in range(trace_len, dof):
        last = dof - height
        starts = [min(trace_len * k // 16 * 16, last) for k in range(6)]
        if last % 16 == 0 and all(
            start + height >= trace_len * (k + 1) for k, start in enumerate(starts)
        ):
            return height, last
    return dof, 0


def lane_tables(trace_len):
    forward, backward = orient_tables(EDGE, COMP)
    gap = LANES - trace_len
    spare = np.arange(trace_len, LANES)
    lanes = np.arange(LANES)
    _, last = window_rows(trace_len)
    into = np.zeros((6 * 8, LANES), np.int32)
    window = np.zeros((6 * 8, LANES), np.int32)
    outof = np.zeros((6 * 8, LANES), np.int32)
    for k in range(6):
        start = min(trace_len * k // 16 * 16, last)
        for code in range(8):
            full = np.concatenate([forward[code], spare])
            into[k * 8 + code] = full[(lanes + gap * k) % LANES]
            window[k * 8 + code] = full[(lanes - (trace_len * k - start)) % LANES]
            full = np.concatenate([backward[code], spare])
            outof[k * 8 + code] = (full - gap * k) % LANES
    return np.stack([into, window, outof])


def swap_routes(devices):
    routes = [[(i, i ^ 1) for i in range(devices)]]
    for shift in (0, 2):
        route = []
        for i in range(devices):
            other = ((i - shift) ^ 3) + shift
            route.append((i, other if i >= shift and other < devices else i ^ 1))
        routes.append(route)
    return routes


def partners(me):
    core = me & 1
    odd_chip = (me >> 1) & 1
    return (
        me ^ 1,
        me + 2 - 4 * odd_chip,
        me - 2 + 4 * odd_chip,
        me - 1 + 2 * core,
    )


def arrivals(me, from_sib, from_even, from_odd):
    shape = from_sib.shape[1:]
    by_even = jnp.broadcast_to(((me ^ (me >> 1)) & 1) == 1, shape)
    return [
        [from_sib[r] for r in range(SLOT)],
        [from_even[SLOT + r] for r in range(SLOT)],
        [from_odd[SLOT + r] for r in range(SLOT)],
        [jnp.where(by_even, from_even[r], from_odd[r]) for r in range(SLOT)],
    ]


def start_all(pairs, sems):
    copies = [
        pltpu.make_async_copy(src, dst, sems.at[i]) for i, (src, dst) in enumerate(pairs)
    ]
    for copy in copies:
        copy.start()
    return copies


def permuted(tile, index):
    index = jnp.broadcast_to(index, tile.shape)
    return jnp.take_along_axis(tile, index, axis=1, mode="promise_in_bounds")


def wanted_faces(me, elem_cap, devices, face_dev, faces, counts):
    width = 2 * LANES
    start = (me - 2) * elem_cap
    block = jnp.clip(start // LANES, 0, faces.shape[1] // LANES - 2)
    window = faces[:, pl.ds(pl.multiple_of(block * LANES, LANES), width)]
    shift = block * LANES - start
    window = pltpu.roll(
        jnp.concatenate([window, window[:2]]), jnp.where(shift < 0, shift + width, shift), 1
    )
    lane = lax.broadcasted_iota(jnp.int32, (1, LANES), 1)
    span = sum((lane >= elem_cap * q).astype(jnp.int32) for q in range(1, 6))
    elem = lane - elem_cap * span
    limit = jnp.zeros_like(lane)
    for q in (0, 1, 3, 4):
        device = me + q - 2
        inside = (device >= 0) & (device < devices)
        count = jnp.where(inside, counts[jnp.clip(device, 0, devices - 1)], 0)
        limit = jnp.where(span == q, count, limit)
    local = [(window[k : k + 1, :LANES] - me * face_dev) for k in range(6)]
    hits = [(x >= 0) & (x < face_dev) & (elem < limit) for x in local]
    ones = [hit.astype(jnp.float32) for hit in hits]
    column = sum(ones)
    before = jnp.broadcast_to(column, (8, LANES))
    elems = jnp.broadcast_to(elem, (8, LANES))
    step = 1
    while step < elem_cap:
        before = before + jnp.where(elems >= step, pltpu.roll(before, step, 1), 0.0)
        step *= 2
    rank = before[:1] - column
    found = [jnp.zeros((1, LANES), jnp.float32) for _ in range(SLOT)]
    for k in range(6):
        value = jnp.where(hits[k], local[k].astype(jnp.float32), 0.0)
        for r in range(SLOT):
            found[r] = found[r] + jnp.where(rank == r, value, 0.0)
        rank = rank + ones[k]
    slots = []
    for device in partners(me):
        inside = (device >= 0) & (device < devices)
        for r in range(SLOT):
            slot = jnp.sum(jnp.where(span == device - me + 2, found[r], 0.0)).astype(jnp.int32)
            slots.append(jnp.where(inside, slot, face_dev))
    return slots


def first_kernel(
    elem_cap,
    devices,
    faces_hbm,
    counts_hbm,
    rhs_hbm,
    blocks_hbm,
    traces,
    rounded,
    swap,
    cross,
    slots,
    faces,
    counts,
    rhs,
    blocks,
    sems,
):
    me = lax.axis_index("elem")
    face_dev, functionals, trace_len = rhs.shape
    copies = start_all(
        [(faces_hbm, faces), (counts_hbm, counts), (rhs_hbm, rhs), (blocks_hbm, blocks)], sems
    )
    copies[0].wait()
    copies[1].wait()
    picked = wanted_faces(me, elem_cap, devices, face_dev, faces, counts)
    for i, slot in enumerate(picked):
        slots[i : i + 1, :] = jnp.full((1, LANES), slot)
    copies[2].wait()
    copies[3].wait()
    for f in range(face_dev):
        value = jnp.dot(rhs[f], blocks[f], preferred_element_type=jnp.float32)
        traces[f] = jnp.zeros((functionals, LANES), jnp.float32)
        traces[f, :, :trace_len] = value
        rounded[f] = traces[f].astype(jnp.bfloat16)
    for group in range(4):
        for r in range(SLOT):
            slot = picked[group * SLOT + r]
            tile = rounded[jnp.where(slot < face_dev, slot, 0)]
            if group == CROSS:
                cross[r] = tile
            else:
                swap[group * SLOT + r] = tile


def home_kernel(
    elem_cap,
    faces_hbm,
    orient_hbm,
    counts_hbm,
    tables_hbm,
    rounded,
    from_sib,
    mats,
    home,
    remote,
    index_in,
    index_out,
    terms,
    faces,
    orient,
    counts,
    tables,
    table,
    rows,
    heads,
    sems,
):
    me = lax.axis_index("elem")
    face_dev, functionals, _ = rounded.shape
    live = elem_cap - elem_cap // 4
    trace_len = mats.shape[1] // 6
    gap = LANES - trace_len
    far = 4 * SLOT
    copies = start_all(
        [(faces_hbm, faces), (orient_hbm, orient), (counts_hbm, counts), (tables_hbm, tables)], sems
    )
    table[:face_dev] = rounded[...]
    table[face_dev] = jnp.zeros((functionals, LANES), jnp.bfloat16)
    table[face_dev + 1 :] = from_sib[:SLOT]
    for copy in copies:
        copy.wait()
    groups = list(partners(me))
    for group, device in enumerate(groups):
        heads[device - me + 2] = group * SLOT
    heads[2] = 0
    index_in[...] = jnp.zeros_like(index_in)
    remote[...] = jnp.full(remote.shape, live * 8)
    count = counts[me]
    magic = (1 << 16) // face_dev + 1
    places = []
    picks = []
    for e in range(live):
        for k in range(6):
            rel = faces[k, me * elem_cap + e] - (me - 2) * face_dev
            used = e < count
            rel = jnp.where(used, rel, 2 * face_dev)
            owner = (rel * magic) >> 16
            head = heads[owner]
            heads[owner] = head + 1
            at_home = owner == 2
            place = jnp.where(at_home & used, rel - 2 * face_dev, face_dev)
            home[6 * e + k] = place
            slot = jnp.where(at_home, far, head)
            places.append(jnp.where(slot < SLOT, face_dev + 1 + slot, place))
            remote[pl.ds(slot, 1), :] = jnp.full((1, LANES), e * 8 + k)
            pick = k * 8 + orient[k, me * elem_cap + e]
            picks.append(pick)
            index_in[pl.ds(slot, 1), :] = tables[1, pl.ds(pick, 1), :]
            index_out[pl.ds(6 * e + k, 1), :] = tables[2, pl.ds(pick, 1), :]
    lane = lax.broadcasted_iota(jnp.int32, (functionals, LANES), 1)
    for e in range(live):
        parts = [
            permuted(
                table[places[6 * e + k]].astype(jnp.float32),
                tables[0, pl.ds(picks[6 * e + k], 1), :],
            )
            for k in range(6)
        ]
        for k in range(6):
            later = parts[k + 1] if k < 5 else jnp.zeros_like(parts[k])
            merged = jnp.where(lane < trace_len - gap * k, parts[k], later)
            rows[e, :, k * LANES : (k + 1) * LANES] = merged.astype(jnp.bfloat16)
    for e in range(live):
        terms[e, :, : 6 * trace_len] = jnp.dot(
            rows[e, :, : 6 * trace_len], mats[e], preferred_element_type=jnp.float32
        )


def remote_kernel(
    remote,
    index_in,
    index_out,
    from_sib,
    from_even,
    from_odd,
    before,
    mats,
    swap,
    cross,
    terms,
):
    me = lax.axis_index("elem")
    functionals = before.shape[1]
    live = before.shape[0]
    trace_len = mats.shape[1] // 6
    gap = LANES - trace_len
    height, last = window_rows(trace_len)
    terms[:live] = before[...]
    terms[live] = jnp.zeros(terms.shape[1:], jnp.float32)
    lane = lax.broadcasted_iota(jnp.int32, (functionals, LANES), 1)
    arrived = arrivals(me, from_sib, from_even, from_odd)
    turned = [
        permuted(arrived[t // SLOT][t % SLOT].astype(jnp.float32), index_in[t : t + 1, :])
        for t in range(4 * SLOT)
    ]
    packs = remote[...]
    where = []
    for group in range(4):
        for r in range(SLOT):
            t = group * SLOT + r
            packed = packs[t, 0]
            e, k = packed >> 3, packed & 7
            where.append((e, k))
            if group == SIB:
                continue
            start = jnp.minimum((trace_len * k) >> 4 << 4, last)
            shift = trace_len * k - start
            tile = turned[t]
            zero = jnp.zeros_like(tile)
            wide = jnp.concatenate(
                [
                    jnp.where((lane >= shift) & (lane < shift + trace_len), tile, zero),
                    jnp.where(lane < shift - gap, tile, zero),
                ],
                axis=1,
            ).astype(jnp.bfloat16)
            window = mats[jnp.minimum(e, live - 1), pl.ds(pl.multiple_of(start, 16), height), :]
            terms[e, :, : 6 * trace_len] += jnp.dot(
                wide[:, :height], window, preferred_element_type=jnp.float32
            )
    for group in range(4):
        for r in range(SLOT):
            t = group * SLOT + r
            e, k = where[t]
            tile = terms[e, :, pl.ds(pl.multiple_of(k * LANES, LANES), LANES)]
            ahead = jnp.maximum(k - 1, 0)
            left = terms[e, :, pl.ds(pl.multiple_of(ahead * LANES, LANES), LANES)]
            tile = jnp.where(lane >= LANES - gap * k, left, tile)
            pick = jnp.minimum(6 * e + k, 6 * live - 1)
            tile = permuted(tile, index_out[pl.ds(pick, 1), :]).astype(jnp.bfloat16)
            if group == CROSS:
                cross[r] = tile
            else:
                swap[group * SLOT + r] = tile


def scatter_kernel(home, index_out, terms, rhs, base):
    face_dev, functionals, trace_len = rhs.shape
    live = terms.shape[0] - 1
    gap = LANES - trace_len
    lane = lax.broadcasted_iota(jnp.int32, (functionals, LANES), 1)
    base[:face_dev, :, :trace_len] = rhs[...].astype(jnp.float32)
    base[face_dev] = jnp.zeros((functionals, LANES), jnp.float32)
    for e in range(live):
        for k in range(6):
            tile = terms[e, :, k * LANES : (k + 1) * LANES]
            if k:
                left = terms[e, :, (k - 1) * LANES : k * LANES]
                tile = jnp.where(lane >= LANES - gap * k, left, tile)
            i = 6 * e + k
            tile = permuted(tile, index_out[i : i + 1, :])
            place = home[i]
            base[place] -= tile.astype(jnp.bfloat16).astype(jnp.float32)


def last_kernel(slots, base, from_sib, from_even, from_odd, blocks, traces, out, residual):
    me = lax.axis_index("elem")
    face_dev, _, trace_len = out.shape
    residual[...] = base[...]
    arrived = arrivals(me, from_sib, from_even, from_odd)
    places = slots[...]
    for group in range(4):
        for r in range(SLOT):
            place = places[group * SLOT + r, 0]
            residual[place] -= arrived[group][r].astype(jnp.float32)
    for f in range(face_dev):
        update = jnp.dot(
            residual[f, :, :trace_len].astype(jnp.bfloat16),
            blocks[f],
            preferred_element_type=jnp.float32,
        )
        out[f] = traces[f, :, :trace_len] + update


def exchange(routes, swap, cross):
    sibling, even_chips, odd_chips = routes
    got = lax.ppermute(swap, "elem", sibling)
    even = jnp.concatenate([cross, got[SLOT : 2 * SLOT]])
    odd = jnp.concatenate([cross, got[2 * SLOT :]])
    return got, lax.ppermute(even, "elem", even_chips), lax.ppermute(odd, "elem", odd_chips)


def per_device(devices, elem_mats, face_blocks, rhs, elem_faces, orient, counts):
    elem_cap, dof, _ = elem_mats.shape
    face_dev, functionals, trace_len = rhs.shape
    live = elem_cap - elem_cap // 4
    far = 4 * SLOT
    routes = swap_routes(devices)

    def in_hbm(array):
        return pltpu.with_memory_space_constraint(array, pltpu.HBM)

    def in_vmem(array):
        return pltpu.with_memory_space_constraint(array, pltpu.VMEM)

    faces = in_hbm(elem_faces.T)
    codes = in_hbm(orient.T)
    counts = in_hbm(counts)
    tables = lane_tables(trace_len)
    vmem = pl.BlockSpec(memory_space=pltpu.VMEM)
    smem = pl.BlockSpec(memory_space=pltpu.SMEM)
    hbm = pl.BlockSpec(memory_space=pltpu.HBM)

    def tiles(count, kind, width=LANES):
        return jax.ShapeDtypeStruct((count, functionals, width), kind)

    def integers(*shape):
        return jax.ShapeDtypeStruct(shape, jnp.int32)

    params = pltpu.CompilerParams(vmem_limit_bytes=4 << 20)
    faces_smem = pltpu.SMEM(faces.shape, jnp.int32)
    counts_smem = pltpu.SMEM(counts.shape, jnp.int32)
    traces, rounded, swap, cross, slots = pl.pallas_call(
        functools.partial(first_kernel, elem_cap, devices),
        out_shape=(
            tiles(face_dev, jnp.float32),
            tiles(face_dev, jnp.bfloat16),
            tiles(3 * SLOT, jnp.bfloat16),
            tiles(SLOT, jnp.bfloat16),
            integers(far, LANES),
        ),
        in_specs=[hbm] * 4,
        out_specs=(vmem,) * 5,
        scratch_shapes=[
            pltpu.VMEM(faces.shape, jnp.int32),
            counts_smem,
            pltpu.VMEM(rhs.shape, rhs.dtype),
            pltpu.VMEM(face_blocks.shape, face_blocks.dtype),
            pltpu.SemaphoreType.DMA((4,)),
        ],
        compiler_params=params,
        cost_estimate=pl.CostEstimate(
            flops=10**11, bytes_accessed=10**8, transcendentals=0
        ),
        name="first_sweep",
    )(faces, counts, in_hbm(rhs), in_hbm(face_blocks))
    from_sib, from_even, from_odd = exchange(routes, swap, cross)
    home, remote, index_in, index_out, terms = pl.pallas_call(
        functools.partial(home_kernel, elem_cap),
        out_shape=(
            integers(6 * live),
            integers(far + 1, LANES),
            integers(far + 1, LANES),
            integers(6 * live, LANES),
            tiles(live, jnp.float32, 6 * LANES),
        ),
        in_specs=[hbm] * 4 + [vmem] * 3,
        out_specs=(smem,) + (vmem,) * 4,
        scratch_shapes=[
            faces_smem,
            faces_smem,
            counts_smem,
            pltpu.VMEM(tables.shape, jnp.int32),
            pltpu.VMEM((face_dev + 1 + SLOT, functionals, LANES), jnp.bfloat16),
            pltpu.VMEM((live, functionals, 6 * LANES), jnp.bfloat16),
            pltpu.SMEM((8,), jnp.int32),
            pltpu.SemaphoreType.DMA((4,)),
        ],
        compiler_params=params,
        cost_estimate=pl.CostEstimate(
            flops=2 * live * functionals * dof * dof,
            bytes_accessed=2 * live * dof * dof,
            transcendentals=0,
        ),
        name="home_terms",
    )(faces, codes, counts, in_hbm(jnp.asarray(tables)), rounded, from_sib, in_vmem(elem_mats))
    swap, cross, terms = pl.pallas_call(
        remote_kernel,
        out_shape=(
            tiles(3 * SLOT, jnp.bfloat16),
            tiles(SLOT, jnp.bfloat16),
            tiles(live + 1, jnp.float32, 6 * LANES),
        ),
        in_specs=[vmem] * 8,
        out_specs=(vmem,) * 3,
        compiler_params=params,
        name="remote_terms",
    )(remote, index_in, index_out, from_sib, from_even, from_odd, terms, in_vmem(elem_mats))
    from_sib, from_even, from_odd = exchange(routes, swap, cross)
    base = pl.pallas_call(
        scatter_kernel,
        out_shape=tiles(face_dev + 1, jnp.float32),
        in_specs=[smem] + [vmem] * 3,
        out_specs=vmem,
        compiler_params=params,
        name="home_sum",
    )(home, index_out, terms, rhs)
    return pl.pallas_call(
        last_kernel,
        out_shape=jax.ShapeDtypeStruct(rhs.shape, jnp.float32),
        in_specs=[vmem] * 7,
        out_specs=vmem,
        scratch_shapes=[
            pltpu.VMEM((face_dev + 1, functionals, LANES), jnp.float32),
        ],
        compiler_params=params,
        name="last_update",
    )(slots, base, from_sib, from_even, from_odd, face_blocks, traces)


def solution(mesh):
    in_specs = (P("elem", None, None), P("elem", None, None), P("elem", None, None), P(), P(), P())
    out_specs = P("elem", None, None)
    return jax.shard_map(
        functools.partial(per_device, mesh.shape["elem"]),
        mesh=mesh,
        in_specs=in_specs,
        out_specs=out_specs,
        check_vma=False,
    )
```

```python
import functools

import jax
import jax.numpy as jnp
import numpy as np
from jax import lax
from jax.experimental import pallas as pl
from jax.experimental.pallas import tpu as pltpu
from jax.sharding import PartitionSpec as P

COMP = 5
EDGE = 5
SLOT = 4
LANES = 128
SIB, EVEN, ODD, CROSS = range(4)


def orient_tables(edge_nodes, components):
    node_ids = np.arange(edge_nodes * edge_nodes)
    row_pos = node_ids // edge_nodes
    col_pos = node_ids % edge_nodes
    table_rows = []
    for orient_code in range(8):
        if orient_code & 4:
            first_pos, second_pos = (col_pos, row_pos)
        else:
            first_pos, second_pos = (row_pos, col_pos)
        if orient_code & 1:
            first_pos = edge_nodes - 1 - first_pos
        if orient_code & 2:
            second_pos = edge_nodes - 1 - second_pos
        moved_node = first_pos * edge_nodes + second_pos
        table_rows.append(
            np.concatenate(
                [
                    part_index * edge_nodes * edge_nodes + moved_node
                    for part_index in range(components)
                ]
            )
        )
    forward = np.stack(table_rows).astype(np.int32)
    backward = np.argsort(forward, axis=1).astype(np.int32)
    return (forward, backward)


def window_rows(trace_len):
    dof = 6 * trace_len
    for height in range(trace_len, dof):
        last = dof - height
        starts = [min(trace_len * k // 16 * 16, last) for k in range(6)]
        if last % 16 == 0 and all(
            start + height >= trace_len * (k + 1) for k, start in enumerate(starts)
        ):
            return height, last
    return dof, 0


def lane_tables(trace_len):
    forward, backward = orient_tables(EDGE, COMP)
    gap = LANES - trace_len
    spare = np.arange(trace_len, LANES)
    lanes = np.arange(LANES)
    _, last = window_rows(trace_len)
    into = np.zeros((6 * 8, LANES), np.int32)
    window = np.zeros((6 * 8, LANES), np.int32)
    outof = np.zeros((6 * 8, LANES), np.int32)
    for k in range(6):
        start = min(trace_len * k // 16 * 16, last)
        for code in range(8):
            full = np.concatenate([forward[code], spare])
            into[k * 8 + code] = full[(lanes + gap * k) % LANES]
            window[k * 8 + code] = full[(lanes - (trace_len * k - start)) % LANES]
            full = np.concatenate([backward[code], spare])
            outof[k * 8 + code] = (full - gap * k) % LANES
    return np.stack([into, window, outof])


def swap_routes(devices):
    routes = [[(i, i ^ 1) for i in range(devices)]]
    for shift in (0, 2):
        route = []
        for i in range(devices):
            other = ((i - shift) ^ 3) + shift
            route.append((i, other if i >= shift and other < devices else i ^ 1))
        routes.append(route)
    return routes


def partners(me):
    core = me & 1
    odd_chip = (me >> 1) & 1
    return (
        me ^ 1,
        me + 2 - 4 * odd_chip,
        me - 2 + 4 * odd_chip,
        me - 1 + 2 * core,
    )


def arrivals(me, from_sib, from_even, from_odd):
    shape = from_sib.shape[1:]
    by_even = jnp.broadcast_to(((me ^ (me >> 1)) & 1) == 1, shape)
    return [
        [from_sib[r] for r in range(SLOT)],
        [from_even[SLOT + r] for r in range(SLOT)],
        [from_odd[SLOT + r] for r in range(SLOT)],
        [jnp.where(by_even, from_even[r], from_odd[r]) for r in range(SLOT)],
    ]


def start_all(pairs, sems):
    copies = [
        pltpu.make_async_copy(src, dst, sems.at[i]) for i, (src, dst) in enumerate(pairs)
    ]
    for copy in copies:
        copy.start()
    return copies


def permuted(tile, index):
    index = jnp.broadcast_to(index, tile.shape)
    return jnp.take_along_axis(tile, index, axis=1, mode="promise_in_bounds")


def lanes_from(array, start):
    width = 2 * LANES
    block = jnp.clip(start // LANES, 0, array.shape[1] // LANES - 2)
    window = array[:, pl.ds(pl.multiple_of(block * LANES, LANES), width)]
    shift = block * LANES - start
    window = jnp.concatenate([window, window[:2]])
    return pltpu.roll(window, jnp.where(shift < 0, shift + width, shift), 1)[:, :LANES]


def sum_before(counts, elem, elem_cap):
    elem = jnp.broadcast_to(elem, counts.shape)
    total = counts
    step = 1
    while step < elem_cap:
        total = total + jnp.where(elem >= step, pltpu.roll(total, step, 1), 0.0)
        step *= 2
    return total - counts


def wanted_faces(me, elem_cap, devices, face_dev, faces, counts):
    window = lanes_from(faces, (me - 2) * elem_cap)
    lane = lax.broadcasted_iota(jnp.int32, (1, LANES), 1)
    span = sum((lane >= elem_cap * q).astype(jnp.int32) for q in range(1, 6))
    elem = lane - elem_cap * span
    limit = jnp.zeros_like(lane)
    for q in (0, 1, 3, 4):
        device = me + q - 2
        inside = (device >= 0) & (device < devices)
        count = jnp.where(inside, counts[jnp.clip(device, 0, devices - 1)], 0)
        limit = jnp.where(span == q, count, limit)
    local = [(window[k : k + 1] - me * face_dev) for k in range(6)]
    hits = [(x >= 0) & (x < face_dev) & (elem < limit) for x in local]
    ones = [hit.astype(jnp.float32) for hit in hits]
    column = sum(ones)
    rank = sum_before(jnp.broadcast_to(column, (8, LANES)), elem, elem_cap)[:1]
    found = [jnp.zeros((1, LANES), jnp.float32) for _ in range(SLOT)]
    for k in range(6):
        value = jnp.where(hits[k], local[k].astype(jnp.float32), 0.0)
        for r in range(SLOT):
            found[r] = found[r] + jnp.where(rank == r, value, 0.0)
        rank = rank + ones[k]
    slots = []
    for device in partners(me):
        inside = (device >= 0) & (device < devices)
        for r in range(SLOT):
            slot = jnp.sum(jnp.where(span == device - me + 2, found[r], 0.0)).astype(jnp.int32)
            slots.append(jnp.where(inside, slot, face_dev))
    return slots


def first_kernel(
    elem_cap,
    devices,
    faces_hbm,
    counts_hbm,
    rhs_hbm,
    blocks_hbm,
    traces,
    rounded,
    swap,
    cross,
    slots,
    faces,
    counts,
    rhs,
    blocks,
    sems,
):
    me = lax.axis_index("elem")
    face_dev, functionals, trace_len = rhs.shape
    copies = start_all(
        [(faces_hbm, faces), (counts_hbm, counts), (rhs_hbm, rhs), (blocks_hbm, blocks)], sems
    )
    copies[0].wait()
    copies[1].wait()
    picked = wanted_faces(me, elem_cap, devices, face_dev, faces, counts)
    for i, slot in enumerate(picked):
        slots[i : i + 1, :] = jnp.full((1, LANES), slot)
    copies[2].wait()
    copies[3].wait()
    for f in range(face_dev):
        value = jnp.dot(rhs[f], blocks[f], preferred_element_type=jnp.float32)
        traces[f] = jnp.zeros((functionals, LANES), jnp.float32)
        traces[f, :, :trace_len] = value
        rounded[f] = traces[f].astype(jnp.bfloat16)
    for group in range(4):
        for r in range(SLOT):
            slot = picked[group * SLOT + r]
            tile = rounded[jnp.where(slot < face_dev, slot, 0)]
            if group == CROSS:
                cross[r] = tile
            else:
                swap[group * SLOT + r] = tile


def own_lists(me, elem_cap, face_dev, faces, orient, counts):
    window = lanes_from(faces, me * elem_cap)
    codes = lanes_from(orient, me * elem_cap)
    lane = lax.broadcasted_iota(jnp.int32, (1, LANES), 1)
    every = lax.broadcasted_iota(jnp.int32, (1, counts.shape[0]), 1)
    count = jnp.sum(jnp.where(every == me, counts[...].reshape(every.shape), 0).astype(jnp.float32))
    used = lane.astype(jnp.float32) < count
    rel = [window[k : k + 1] - (me - 2) * face_dev for k in range(6)]
    owner = [sum((x >= face_dev * j).astype(jnp.int32) for j in range(1, 5)) for x in rel]
    owner = [jnp.where(used, x, 2) for x in owner]
    others = [0, 1, 3, 4]
    column = [sum((x == j).astype(jnp.float32) for x in owner) for j in others]
    column = jnp.concatenate(column + [jnp.zeros((4, LANES), jnp.float32)])
    ranks = sum_before(column, lane, elem_cap).astype(jnp.int32)
    heads = []
    for i, j in enumerate(others):
        base = sum(
            jnp.where(device == me + j - 2, group * SLOT, 0)
            for group, device in enumerate(partners(me))
        )
        heads.append(ranks[i : i + 1] + base)
    gather, home, slots, picks = [], [], [], []
    for k in range(6):
        slot = jnp.full_like(lane, 4 * SLOT)
        for i, j in enumerate(others):
            hit = owner[k] == j
            slot = jnp.where(hit, heads[i], slot)
            heads[i] = heads[i] + hit.astype(jnp.int32)
        place = jnp.where(used & (owner[k] == 2), rel[k] - 2 * face_dev, face_dev)
        gather.append(jnp.where(slot < SLOT, face_dev + 1 + slot, place))
        home.append(place)
        slots.append(slot)
        picks.append(codes[k : k + 1] + 8 * k)
    return gather, home, slots, picks


def home_kernel(
    elem_cap,
    faces,
    orient,
    counts,
    tables,
    rounded,
    from_sib,
    mats,
    terms,
    sums,
    remote,
    index_in,
    table,
    rows,
):
    me = lax.axis_index("elem")
    face_dev, functionals, _ = rounded.shape
    live = rows.shape[0]
    trace_len = mats.shape[1] // 6
    gap = LANES - trace_len
    table[:face_dev] = rounded[...]
    table[face_dev] = jnp.zeros((functionals, LANES), jnp.bfloat16)
    table[face_dev + 1 :] = from_sib[:SLOT]
    gather, home, slots, picks = own_lists(me, elem_cap, face_dev, faces, orient, counts)
    packed = [gather[k] * 64 + picks[k] for k in range(6)]
    for k in range(6):
        sums[k : k + 1, :] = home[k] * 64 + picks[k]
    lane = lax.broadcasted_iota(jnp.int32, (functionals, LANES), 1)
    for e in range(live):
        parts = []
        for k in range(6):
            code = packed[k][0, e]
            tile = table[code >> 6].astype(jnp.float32)
            parts.append(permuted(tile, tables[0, pl.ds(code & 63, 1), :]))
        for k in range(6):
            later = parts[k + 1] if k < 5 else jnp.zeros_like(parts[k])
            merged = jnp.where(lane < trace_len - gap * k, parts[k], later)
            rows[e, :, k * LANES : (k + 1) * LANES] = merged.astype(jnp.bfloat16)
    for e in range(live):
        terms[e, :, : 6 * trace_len] = jnp.dot(
            rows[e, :, : 6 * trace_len], mats[e], preferred_element_type=jnp.float32
        )
    elem = lax.broadcasted_iota(jnp.int32, (1, LANES), 1)
    for t in range(4 * SLOT):
        entry = jnp.zeros((1, LANES), jnp.float32)
        for k in range(6):
            code = ((elem - live) * 8 + k) * 64 + picks[k]
            entry = entry + jnp.where(slots[k] == t, code.astype(jnp.float32), 0.0)
        code = jnp.sum(entry).astype(jnp.int32) + live * 512
        remote[t : t + 1, :] = jnp.full((1, LANES), code)
        index_in[t : t + 1, :] = tables[1, pl.ds(code & 63, 1), :]


def remote_kernel(
    remote,
    index_in,
    tables,
    from_sib,
    from_even,
    from_odd,
    before,
    mats,
    swap,
    cross,
    terms,
):
    me = lax.axis_index("elem")
    functionals = before.shape[1]
    live = before.shape[0]
    trace_len = mats.shape[1] // 6
    gap = LANES - trace_len
    height, last = window_rows(trace_len)
    terms[:live] = before[...]
    terms[live] = jnp.zeros(terms.shape[1:], jnp.float32)
    lane = lax.broadcasted_iota(jnp.int32, (functionals, LANES), 1)
    arrived = arrivals(me, from_sib, from_even, from_odd)
    turned = [
        permuted(arrived[t // SLOT][t % SLOT].astype(jnp.float32), index_in[t : t + 1, :])
        for t in range(4 * SLOT)
    ]
    packs = remote[...]
    where = []
    for group in range(4):
        for r in range(SLOT):
            t = group * SLOT + r
            packed = packs[t, 0]
            e, k = packed >> 9, (packed >> 6) & 7
            where.append((e, k, packed & 63))
            if group == SIB:
                continue
            start = jnp.minimum((trace_len * k) >> 4 << 4, last)
            shift = trace_len * k - start
            tile = turned[t]
            zero = jnp.zeros_like(tile)
            wide = jnp.concatenate(
                [
                    jnp.where((lane >= shift) & (lane < shift + trace_len), tile, zero),
                    jnp.where(lane < shift - gap, tile, zero),
                ],
                axis=1,
            ).astype(jnp.bfloat16)
            window = mats[jnp.minimum(e, live - 1), pl.ds(pl.multiple_of(start, 16), height), :]
            terms[e, :, : 6 * trace_len] += jnp.dot(
                wide[:, :height], window, preferred_element_type=jnp.float32
            )
    for group in range(4):
        for r in range(SLOT):
            t = group * SLOT + r
            e, k, pick = where[t]
            tile = terms[e, :, pl.ds(pl.multiple_of(k * LANES, LANES), LANES)]
            ahead = jnp.maximum(k - 1, 0)
            left = terms[e, :, pl.ds(pl.multiple_of(ahead * LANES, LANES), LANES)]
            tile = jnp.where(lane >= LANES - gap * k, left, tile)
            tile = permuted(tile, tables[2, pl.ds(pick, 1), :]).astype(jnp.bfloat16)
            if group == CROSS:
                cross[r] = tile
            else:
                swap[group * SLOT + r] = tile


def scatter_kernel(sums, tables, terms, rhs, base):
    face_dev, functionals, trace_len = rhs.shape
    live = terms.shape[0] - 1
    gap = LANES - trace_len
    lane = lax.broadcasted_iota(jnp.int32, (functionals, LANES), 1)
    base[:face_dev, :, :trace_len] = rhs[...].astype(jnp.float32)
    base[face_dev] = jnp.zeros((functionals, LANES), jnp.float32)
    codes = sums[...]
    for e in range(live):
        for k in range(6):
            tile = terms[e, :, k * LANES : (k + 1) * LANES]
            if k:
                left = terms[e, :, (k - 1) * LANES : k * LANES]
                tile = jnp.where(lane >= LANES - gap * k, left, tile)
            code = codes[k, e]
            tile = permuted(tile, tables[2, pl.ds(code & 63, 1), :])
            place = code >> 6
            base[place] -= tile.astype(jnp.bfloat16).astype(jnp.float32)


def last_kernel(slots, base, from_sib, from_even, from_odd, blocks, traces, out, residual):
    me = lax.axis_index("elem")
    face_dev, _, trace_len = out.shape
    residual[...] = base[...]
    arrived = arrivals(me, from_sib, from_even, from_odd)
    places = slots[...]
    for group in range(4):
        for r in range(SLOT):
            place = places[group * SLOT + r, 0]
            residual[place] -= arrived[group][r].astype(jnp.float32)
    for f in range(face_dev):
        update = jnp.dot(
            residual[f, :, :trace_len].astype(jnp.bfloat16),
            blocks[f],
            preferred_element_type=jnp.float32,
        )
        out[f] = traces[f, :, :trace_len] + update


def exchange(routes, swap, cross):
    sibling, even_chips, odd_chips = routes
    got = lax.ppermute(swap, "elem", sibling)
    even = jnp.concatenate([cross, got[SLOT : 2 * SLOT]])
    odd = jnp.concatenate([cross, got[2 * SLOT :]])
    return got, lax.ppermute(even, "elem", even_chips), lax.ppermute(odd, "elem", odd_chips)


def per_device(devices, elem_mats, face_blocks, rhs, elem_faces, orient, counts):
    elem_cap, dof, _ = elem_mats.shape
    face_dev, functionals, trace_len = rhs.shape
    live = elem_cap - elem_cap // 4
    far = 4 * SLOT
    routes = swap_routes(devices)

    def in_hbm(array):
        return pltpu.with_memory_space_constraint(array, pltpu.HBM)

    def in_vmem(array):
        return pltpu.with_memory_space_constraint(array, pltpu.VMEM)

    faces = in_hbm(elem_faces.T)
    tables = jnp.asarray(lane_tables(trace_len))
    vmem = pl.BlockSpec(memory_space=pltpu.VMEM)
    smem = pl.BlockSpec(memory_space=pltpu.SMEM)
    hbm = pl.BlockSpec(memory_space=pltpu.HBM)

    def tiles(count, kind, width=LANES):
        return jax.ShapeDtypeStruct((count, functionals, width), kind)

    def integers(*shape):
        return jax.ShapeDtypeStruct(shape, jnp.int32)

    params = pltpu.CompilerParams(vmem_limit_bytes=4 << 20)
    counts_smem = pltpu.SMEM(counts.shape, jnp.int32)
    traces, rounded, swap, cross, slots = pl.pallas_call(
        functools.partial(first_kernel, elem_cap, devices),
        out_shape=(
            tiles(face_dev, jnp.float32),
            tiles(face_dev, jnp.bfloat16),
            tiles(3 * SLOT, jnp.bfloat16),
            tiles(SLOT, jnp.bfloat16),
            integers(far, LANES),
        ),
        in_specs=[hbm] * 4,
        out_specs=(vmem,) * 5,
        scratch_shapes=[
            pltpu.VMEM(faces.shape, jnp.int32),
            counts_smem,
            pltpu.VMEM(rhs.shape, rhs.dtype),
            pltpu.VMEM(face_blocks.shape, face_blocks.dtype),
            pltpu.SemaphoreType.DMA((4,)),
        ],
        compiler_params=params,
        cost_estimate=pl.CostEstimate(
            flops=10**11, bytes_accessed=10**8, transcendentals=0
        ),
        name="first_sweep",
    )(faces, in_hbm(counts), in_hbm(rhs), in_hbm(face_blocks))
    from_sib, from_even, from_odd = exchange(routes, swap, cross)
    terms, sums, remote, index_in = pl.pallas_call(
        functools.partial(home_kernel, elem_cap),
        out_shape=(
            tiles(live, jnp.float32, 6 * LANES),
            integers(6, LANES),
            integers(far, LANES),
            integers(far, LANES),
        ),
        in_specs=[vmem] * 7,
        out_specs=(vmem,) * 4,
        scratch_shapes=[
            pltpu.VMEM((face_dev + 1 + SLOT, functionals, LANES), jnp.bfloat16),
            pltpu.VMEM((live, functionals, 6 * LANES), jnp.bfloat16),
        ],
        compiler_params=params,
        cost_estimate=pl.CostEstimate(
            flops=2 * live * functionals * dof * dof,
            bytes_accessed=2 * live * dof * dof,
            transcendentals=0,
        ),
        name="home_terms",
    )(elem_faces.T, orient.T, counts, tables, rounded, from_sib, in_vmem(elem_mats))
    swap, cross, terms = pl.pallas_call(
        remote_kernel,
        out_shape=(
            tiles(3 * SLOT, jnp.bfloat16),
            tiles(SLOT, jnp.bfloat16),
            tiles(live + 1, jnp.float32, 6 * LANES),
        ),
        in_specs=[vmem] * 8,
        out_specs=(vmem,) * 3,
        compiler_params=params,
        name="remote_terms",
    )(remote, index_in, tables, from_sib, from_even, from_odd, terms, in_vmem(elem_mats))
    from_sib, from_even, from_odd = exchange(routes, swap, cross)
    base = pl.pallas_call(
        scatter_kernel,
        out_shape=tiles(face_dev + 1, jnp.float32),
        in_specs=[vmem] * 4,
        out_specs=vmem,
        compiler_params=params,
        name="home_sum",
    )(sums, tables, terms, rhs)
    return pl.pallas_call(
        last_kernel,
        out_shape=jax.ShapeDtypeStruct(rhs.shape, jnp.float32),
        in_specs=[vmem] * 7,
        out_specs=vmem,
        scratch_shapes=[
            pltpu.VMEM((face_dev + 1, functionals, LANES), jnp.float32),
        ],
        compiler_params=params,
        name="last_update",
    )(slots, base, from_sib, from_even, from_odd, face_blocks, traces)


def solution(mesh):
    in_specs = (P("elem", None, None), P("elem", None, None), P("elem", None, None), P(), P(), P())
    out_specs = P("elem", None, None)
    return jax.shard_map(
        functools.partial(per_device, mesh.shape["elem"]),
        mesh=mesh,
        in_specs=in_specs,
        out_specs=out_specs,
        check_vma=False,
    )
```

```python
import functools

import jax
import jax.numpy as jnp
import numpy as np
from jax import lax
from jax.experimental import pallas as pl
from jax.experimental.pallas import tpu as pltpu
from jax.sharding import PartitionSpec as P

COMP = 5
EDGE = 5
SLOT = 4
LANES = 128
SIB, EVEN, ODD, CROSS = range(4)


def orient_tables(edge_nodes, components):
    node_ids = np.arange(edge_nodes * edge_nodes)
    row_pos = node_ids // edge_nodes
    col_pos = node_ids % edge_nodes
    table_rows = []
    for orient_code in range(8):
        if orient_code & 4:
            first_pos, second_pos = (col_pos, row_pos)
        else:
            first_pos, second_pos = (row_pos, col_pos)
        if orient_code & 1:
            first_pos = edge_nodes - 1 - first_pos
        if orient_code & 2:
            second_pos = edge_nodes - 1 - second_pos
        moved_node = first_pos * edge_nodes + second_pos
        table_rows.append(
            np.concatenate(
                [
                    part_index * edge_nodes * edge_nodes + moved_node
                    for part_index in range(components)
                ]
            )
        )
    forward = np.stack(table_rows).astype(np.int32)
    backward = np.argsort(forward, axis=1).astype(np.int32)
    return (forward, backward)


def window_rows(trace_len):
    dof = 6 * trace_len
    for height in range(trace_len, dof):
        last = dof - height
        starts = [min(trace_len * k // 16 * 16, last) for k in range(6)]
        if last % 16 == 0 and all(
            start + height >= trace_len * (k + 1) for k, start in enumerate(starts)
        ):
            return height, last
    return dof, 0


def lane_tables(trace_len):
    forward, backward = orient_tables(EDGE, COMP)
    gap = LANES - trace_len
    spare = np.arange(trace_len, LANES)
    lanes = np.arange(LANES)
    _, last = window_rows(trace_len)
    into = np.zeros((6 * 8, LANES), np.int32)
    window = np.zeros((6 * 8, LANES), np.int32)
    outof = np.zeros((6 * 8, LANES), np.int32)
    for k in range(6):
        start = min(trace_len * k // 16 * 16, last)
        for code in range(8):
            full = np.concatenate([forward[code], spare])
            into[k * 8 + code] = full[(lanes + gap * k) % LANES]
            window[k * 8 + code] = full[(lanes - (trace_len * k - start)) % LANES]
            full = np.concatenate([backward[code], spare])
            outof[k * 8 + code] = (full - gap * k) % LANES
    return np.stack([into, window, outof])


def swap_routes(devices):
    routes = [[(i, i ^ 1) for i in range(devices)]]
    for shift in (0, 2):
        route = []
        for i in range(devices):
            other = ((i - shift) ^ 3) + shift
            route.append((i, other if i >= shift and other < devices else i ^ 1))
        routes.append(route)
    return routes


def partners(me):
    core = me & 1
    odd_chip = (me >> 1) & 1
    return (
        me ^ 1,
        me + 2 - 4 * odd_chip,
        me - 2 + 4 * odd_chip,
        me - 1 + 2 * core,
    )


def crossing_bucket(from_even, from_odd):
    me = lax.axis_index("elem")
    by_even = jnp.broadcast_to(((me ^ (me >> 1)) & 1) == 1, from_even.shape[1:])
    return [jnp.where(by_even, from_even[r], from_odd[r]) for r in range(SLOT)]


def put_bucket(group, r, tile, swap, even):
    target, first = {SIB: (swap, 0), ODD: (swap, SLOT), CROSS: (even, 0), EVEN: (even, SLOT)}[group]
    target[first + r] = tile


def start_all(pairs, sems):
    copies = [
        pltpu.make_async_copy(src, dst, sems.at[i]) for i, (src, dst) in enumerate(pairs)
    ]
    for copy in copies:
        copy.start()
    return copies


def permuted(tile, index):
    index = jnp.broadcast_to(index, tile.shape)
    return jnp.take_along_axis(tile, index, axis=1, mode="promise_in_bounds")


def lanes_from(array, start):
    width = 2 * LANES
    block = jnp.clip(start // LANES, 0, array.shape[1] // LANES - 2)
    window = array[:, pl.ds(pl.multiple_of(block * LANES, LANES), width)]
    shift = block * LANES - start
    window = jnp.concatenate([window, window[:2]])
    return pltpu.roll(window, jnp.where(shift < 0, shift + width, shift), 1)[:, :LANES]


def sum_before(counts, elem, elem_cap):
    elem = jnp.broadcast_to(elem, counts.shape)
    total = counts
    step = 1
    while step < elem_cap:
        total = total + jnp.where(elem >= step, pltpu.roll(total, step, 1), 0.0)
        step *= 2
    return total - counts


def wanted_faces(me, elem_cap, devices, face_dev, faces, counts):
    window = lanes_from(faces, (me - 2) * elem_cap)
    lane = lax.broadcasted_iota(jnp.int32, (1, LANES), 1)
    span = sum((lane >= elem_cap * q).astype(jnp.int32) for q in range(1, 6))
    elem = lane - elem_cap * span
    limit = jnp.zeros_like(lane)
    for q in (0, 1, 3, 4):
        device = me + q - 2
        inside = (device >= 0) & (device < devices)
        count = jnp.where(inside, counts[jnp.clip(device, 0, devices - 1)], 0)
        limit = jnp.where(span == q, count, limit)
    local = [(window[k : k + 1] - me * face_dev) for k in range(6)]
    hits = [(x >= 0) & (x < face_dev) & (elem < limit) for x in local]
    ones = [hit.astype(jnp.float32) for hit in hits]
    column = sum(ones)
    rank = sum_before(jnp.broadcast_to(column, (8, LANES)), elem, elem_cap)[:1]
    found = [jnp.zeros((1, LANES), jnp.float32) for _ in range(SLOT)]
    for k in range(6):
        value = jnp.where(hits[k], local[k].astype(jnp.float32), 0.0)
        for r in range(SLOT):
            found[r] = found[r] + jnp.where(rank == r, value, 0.0)
        rank = rank + ones[k]
    slots = []
    for device in partners(me):
        inside = (device >= 0) & (device < devices)
        for r in range(SLOT):
            slot = jnp.sum(jnp.where(span == device - me + 2, found[r], 0.0)).astype(jnp.int32)
            slots.append(jnp.where(inside, slot, face_dev))
    return slots


def first_kernel(
    elem_cap,
    devices,
    faces_hbm,
    counts_hbm,
    rhs_hbm,
    blocks_hbm,
    traces,
    rounded,
    swap,
    even,
    slots,
    faces,
    counts,
    rhs,
    blocks,
    sems,
):
    me = lax.axis_index("elem")
    face_dev, functionals, trace_len = rhs.shape
    copies = start_all(
        [(faces_hbm, faces), (counts_hbm, counts), (rhs_hbm, rhs), (blocks_hbm, blocks)], sems
    )
    copies[0].wait()
    copies[1].wait()
    picked = wanted_faces(me, elem_cap, devices, face_dev, faces, counts)
    for i, slot in enumerate(picked):
        slots[i : i + 1, :] = jnp.full((1, LANES), slot)
    copies[2].wait()
    copies[3].wait()
    for f in range(face_dev):
        value = jnp.dot(rhs[f], blocks[f], preferred_element_type=jnp.float32)
        traces[f, :, :trace_len] = value
        rounded[f, :, :trace_len] = value.astype(jnp.bfloat16)
    for group in range(4):
        for r in range(SLOT):
            slot = picked[group * SLOT + r]
            tile = rounded[jnp.where(slot < face_dev, slot, 0)]
            put_bucket(group, r, tile, swap, even)


def own_lists(me, elem_cap, face_dev, faces, orient, counts):
    window = lanes_from(faces, me * elem_cap)
    codes = lanes_from(orient, me * elem_cap)
    lane = lax.broadcasted_iota(jnp.int32, (1, LANES), 1)
    every = lax.broadcasted_iota(jnp.int32, (1, counts.shape[0]), 1)
    count = jnp.sum(jnp.where(every == me, counts[...].reshape(every.shape), 0).astype(jnp.float32))
    used = lane.astype(jnp.float32) < count
    rel = [window[k : k + 1] - (me - 2) * face_dev for k in range(6)]
    owner = [sum((x >= face_dev * j).astype(jnp.int32) for j in range(1, 5)) for x in rel]
    owner = [jnp.where(used, x, 2) for x in owner]
    others = [0, 1, 3, 4]
    column = [sum((x == j).astype(jnp.float32) for x in owner) for j in others]
    column = jnp.concatenate(column + [jnp.zeros((4, LANES), jnp.float32)])
    ranks = sum_before(column, lane, elem_cap).astype(jnp.int32)
    heads = []
    for i, j in enumerate(others):
        base = sum(
            jnp.where(device == me + j - 2, group * SLOT, 0)
            for group, device in enumerate(partners(me))
        )
        heads.append(ranks[i : i + 1] + base)
    gather, home, slots, picks = [], [], [], []
    for k in range(6):
        slot = jnp.full_like(lane, 4 * SLOT)
        for i, j in enumerate(others):
            hit = owner[k] == j
            slot = jnp.where(hit, heads[i], slot)
            heads[i] = heads[i] + hit.astype(jnp.int32)
        place = jnp.where(used & (owner[k] == 2), rel[k] - 2 * face_dev, face_dev)
        gather.append(jnp.where(slot < SLOT, face_dev + 1 + slot, place))
        home.append(place)
        slots.append(slot)
        picks.append(codes[k : k + 1] + 8 * k)
    return gather, home, slots, picks


def rows_kernel(
    elem_cap,
    faces,
    orient,
    counts,
    tables,
    rounded,
    from_sib,
    rows,
    sums,
    remote,
    index_in,
    table,
):
    me = lax.axis_index("elem")
    face_dev, functionals, _ = rounded.shape
    live = rows.shape[0]
    trace_len = COMP * EDGE * EDGE
    gap = LANES - trace_len
    table[:face_dev] = rounded[...]
    table[face_dev] = jnp.zeros((functionals, LANES), jnp.bfloat16)
    table[face_dev + 1 :] = from_sib[:SLOT]
    gather, home, slots, picks = own_lists(me, elem_cap, face_dev, faces, orient, counts)
    packed = [gather[k] * 64 + picks[k] for k in range(6)]
    for k in range(6):
        sums[k : k + 1, :] = home[k] * 64 + picks[k]
    lane = lax.broadcasted_iota(jnp.int32, (functionals, LANES), 1)
    for e in range(live):
        parts = []
        for k in range(6):
            code = packed[k][0, e]
            tile = table[code >> 6].astype(jnp.float32)
            parts.append(permuted(tile, tables[0, pl.ds(code & 63, 1), :]))
        for k in range(6):
            later = parts[k + 1] if k < 5 else jnp.zeros_like(parts[k])
            merged = jnp.where(lane < trace_len - gap * k, parts[k], later)
            rows[e, :, k * LANES : (k + 1) * LANES] = merged.astype(jnp.bfloat16)
    elem = lax.broadcasted_iota(jnp.int32, (1, LANES), 1)
    for t in range(4 * SLOT):
        entry = jnp.zeros((1, LANES), jnp.float32)
        for k in range(6):
            code = ((elem - live) * 8 + k) * 64 + picks[k]
            entry = entry + jnp.where(slots[k] == t, code.astype(jnp.float32), 0.0)
        code = jnp.sum(entry).astype(jnp.int32) + live * 512
        remote[t : t + 1, :] = jnp.full((1, LANES), code)
        index_in[t : t + 1, :] = tables[1, pl.ds(code & 63, 1), :]


def home_kernel(rows, mats, terms):
    live = rows.shape[0]
    dof = mats.shape[1]
    for e in range(live):
        terms[e, :, :dof] = jnp.dot(rows[e, :, :dof], mats[e], preferred_element_type=jnp.float32)
    terms[live] = jnp.zeros(terms.shape[1:], jnp.float32)


def unpacked(packs, t):
    packed = packs[t, 0]
    return packed >> 9, (packed >> 6) & 7, packed & 63


def add_remote(group, arrived, first, packs, index_in, mats, terms):
    live = terms.shape[0] - 1
    trace_len = mats.shape[1] // 6
    gap = LANES - trace_len
    height, last = window_rows(trace_len)
    lane = lax.broadcasted_iota(jnp.int32, arrived[first].shape, 1)
    for r in range(SLOT):
        t = group * SLOT + r
        e, k, _ = unpacked(packs, t)
        start = jnp.minimum((trace_len * k) >> 4 << 4, last)
        shift = trace_len * k - start
        tile = permuted(arrived[first + r].astype(jnp.float32), index_in[t : t + 1, :])
        zero = jnp.zeros_like(tile)
        wide = jnp.concatenate(
            [
                jnp.where((lane >= shift) & (lane < shift + trace_len), tile, zero),
                jnp.where(lane < shift - gap, tile, zero),
            ],
            axis=1,
        ).astype(jnp.bfloat16)
        window = mats[jnp.minimum(e, live - 1), pl.ds(pl.multiple_of(start, 16), height), :]
        terms[e, :, : 6 * trace_len] += jnp.dot(
            wide[:, :height], window, preferred_element_type=jnp.float32
        )


def relay_kernel(from_even, _, out):
    out[...] = from_even[SLOT:]


def remote_kernel(
    remote, index_in, tables, from_even, from_odd, relayed, mats, _, swap, even, terms
):
    trace_len = mats.shape[1] // 6
    gap = LANES - trace_len
    packs = remote[...]
    add_remote(EVEN, relayed, 0, packs, index_in, mats, terms)
    add_remote(CROSS, crossing_bucket(from_even, from_odd), 0, packs, index_in, mats, terms)
    add_remote(ODD, from_odd, SLOT, packs, index_in, mats, terms)
    lane = lax.broadcasted_iota(jnp.int32, relayed.shape[1:], 1)
    for group in range(4):
        for r in range(SLOT):
            e, k, pick = unpacked(packs, group * SLOT + r)
            tile = terms[e, :, pl.ds(pl.multiple_of(k * LANES, LANES), LANES)]
            ahead = jnp.maximum(k - 1, 0)
            left = terms[e, :, pl.ds(pl.multiple_of(ahead * LANES, LANES), LANES)]
            tile = jnp.where(lane >= LANES - gap * k, left, tile)
            tile = permuted(tile, tables[2, pl.ds(pick, 1), :]).astype(jnp.bfloat16)
            put_bucket(group, r, tile, swap, even)


def scatter_kernel(sums, tables, terms, rhs, base):
    face_dev, functionals, trace_len = rhs.shape
    live = terms.shape[0] - 1
    gap = LANES - trace_len
    lane = lax.broadcasted_iota(jnp.int32, (functionals, LANES), 1)
    base[:face_dev, :, :trace_len] = rhs[...].astype(jnp.float32)
    base[face_dev] = jnp.zeros((functionals, LANES), jnp.float32)
    codes = sums[...]
    for e in range(live):
        for k in range(6):
            tile = terms[e, :, k * LANES : (k + 1) * LANES]
            if k:
                left = terms[e, :, (k - 1) * LANES : k * LANES]
                tile = jnp.where(lane >= LANES - gap * k, left, tile)
            code = codes[k, e]
            tile = permuted(tile, tables[2, pl.ds(code & 63, 1), :])
            place = code >> 6
            base[place] -= tile.astype(jnp.bfloat16).astype(jnp.float32)


def last_kernel(
    slots, base, from_sib, from_even, from_odd, relayed, blocks, traces, out, residual
):
    face_dev, _, trace_len = out.shape
    residual[...] = base[...]
    crossing = crossing_bucket(from_even, from_odd)
    places = slots[...]
    for r in range(SLOT):
        arrived = {SIB: from_sib[r], EVEN: relayed[r], ODD: from_odd[SLOT + r], CROSS: crossing[r]}
        for group, tile in arrived.items():
            place = places[group * SLOT + r, 0]
            residual[place] -= tile.astype(jnp.float32)
    for f in range(face_dev):
        update = jnp.dot(
            residual[f, :, :trace_len].astype(jnp.bfloat16),
            blocks[f],
            preferred_element_type=jnp.float32,
        )
        out[f] = traces[f, :, :trace_len] + update


def exchange(routes, swap, even):
    sibling, even_chips, odd_chips = routes
    from_even = lax.ppermute(even, "elem", even_chips)
    from_sib = lax.ppermute(swap, "elem", sibling)
    odd = jnp.concatenate([even[:SLOT], from_sib[SLOT:]])
    return from_sib, from_even, lax.ppermute(odd, "elem", odd_chips)


def per_device(devices, elem_mats, face_blocks, rhs, elem_faces, orient, counts):
    elem_cap, dof, _ = elem_mats.shape
    face_dev, functionals, trace_len = rhs.shape
    live = elem_cap - elem_cap // 4
    far = 4 * SLOT
    routes = swap_routes(devices)

    def in_hbm(array):
        return pltpu.with_memory_space_constraint(array, pltpu.HBM)

    def in_vmem(array):
        return pltpu.with_memory_space_constraint(array, pltpu.VMEM)

    faces = in_hbm(elem_faces.T)
    tables = jnp.asarray(lane_tables(trace_len))
    vmem = pl.BlockSpec(memory_space=pltpu.VMEM)
    smem = pl.BlockSpec(memory_space=pltpu.SMEM)
    hbm = pl.BlockSpec(memory_space=pltpu.HBM)

    def tiles(count, kind, width=LANES):
        return jax.ShapeDtypeStruct((count, functionals, width), kind)

    def integers(*shape):
        return jax.ShapeDtypeStruct(shape, jnp.int32)

    params = pltpu.CompilerParams(vmem_limit_bytes=4 << 20)
    counts_smem = pltpu.SMEM(counts.shape, jnp.int32)
    traces, rounded, swap, even, slots = pl.pallas_call(
        functools.partial(first_kernel, elem_cap, devices),
        out_shape=(
            tiles(face_dev, jnp.float32),
            tiles(face_dev, jnp.bfloat16),
            tiles(2 * SLOT, jnp.bfloat16),
            tiles(2 * SLOT, jnp.bfloat16),
            integers(far, LANES),
        ),
        in_specs=[hbm] * 4,
        out_specs=(vmem,) * 5,
        scratch_shapes=[
            pltpu.VMEM(faces.shape, jnp.int32),
            counts_smem,
            pltpu.VMEM(rhs.shape, rhs.dtype),
            pltpu.VMEM(face_blocks.shape, face_blocks.dtype),
            pltpu.SemaphoreType.DMA((4,)),
        ],
        compiler_params=params,
        cost_estimate=pl.CostEstimate(
            flops=10**11, bytes_accessed=10**8, transcendentals=0
        ),
        name="first_sweep",
    )(faces, in_hbm(counts), in_hbm(rhs), in_hbm(face_blocks))
    def passed_on(from_even, after):
        relay = pl.pallas_call(
            relay_kernel,
            out_shape=tiles(SLOT, jnp.bfloat16),
            in_specs=[vmem, pl.BlockSpec(memory_space=pl.ANY)],
            out_specs=vmem,
            compiler_params=params,
            name="relay",
        )(from_even, after)
        return lax.ppermute(relay, "elem", routes[0])

    from_sib, from_even, from_odd = exchange(routes, swap, even)
    all_terms = pltpu.VMEM((live + 1, functionals, 6 * LANES), jnp.float32)
    rows, sums, remote, index_in = pl.pallas_call(
        functools.partial(rows_kernel, elem_cap),
        out_shape=(
            tiles(live, jnp.bfloat16, 6 * LANES),
            integers(6, LANES),
            integers(far, LANES),
            integers(far, LANES),
        ),
        in_specs=[vmem] * 6,
        out_specs=(vmem,) * 4,
        scratch_shapes=[pltpu.VMEM((face_dev + 1 + SLOT, functionals, LANES), jnp.bfloat16)],
        compiler_params=params,
        name="home_rows",
    )(elem_faces.T, orient.T, counts, tables, rounded, from_sib)
    terms = pl.pallas_call(
        home_kernel,
        out_shape=all_terms,
        in_specs=[vmem] * 2,
        out_specs=vmem,
        compiler_params=params,
        cost_estimate=pl.CostEstimate(
            flops=2 * live * functionals * dof * dof,
            bytes_accessed=2 * live * dof * dof,
            transcendentals=0,
        ),
        name="home_terms",
    )(rows, in_vmem(elem_mats))
    relayed = passed_on(from_even, sums)
    swap, even, terms = pl.pallas_call(
        remote_kernel,
        out_shape=(tiles(2 * SLOT, jnp.bfloat16), tiles(2 * SLOT, jnp.bfloat16), all_terms),
        in_specs=[vmem] * 8,
        out_specs=(vmem,) * 3,
        input_output_aliases={7: 2},
        compiler_params=params,
        name="remote_terms",
    )(
        remote,
        index_in,
        tables,
        from_even,
        from_odd,
        relayed,
        in_vmem(elem_mats),
        in_vmem(terms),
    )
    from_sib, from_even, from_odd = exchange(routes, swap, even)
    base = pl.pallas_call(
        scatter_kernel,
        out_shape=tiles(face_dev + 1, jnp.float32),
        in_specs=[vmem] * 4,
        out_specs=vmem,
        compiler_params=params,
        name="home_sum",
    )(sums, tables, terms, rhs)
    relayed = passed_on(from_even, base)
    return pl.pallas_call(
        last_kernel,
        out_shape=jax.ShapeDtypeStruct(rhs.shape, jnp.float32),
        in_specs=[vmem] * 8,
        out_specs=vmem,
        scratch_shapes=[
            pltpu.VMEM((face_dev + 1, functionals, LANES), jnp.float32),
        ],
        compiler_params=params,
        name="last_update",
    )(slots, base, from_sib, from_even, from_odd, relayed, face_blocks, traces)


def solution(mesh):
    in_specs = (P("elem", None, None), P("elem", None, None), P("elem", None, None), P(), P(), P())
    out_specs = P("elem", None, None)
    return jax.shard_map(
        functools.partial(per_device, mesh.shape["elem"]),
        mesh=mesh,
        in_specs=in_specs,
        out_specs=out_specs,
        check_vma=False,
    )
```

```python
import functools

import jax
import jax.numpy as jnp
import numpy as np
from jax import lax
from jax.experimental import pallas as pl
from jax.experimental.pallas import tpu as pltpu
from jax.sharding import PartitionSpec as P

COMP = 5
EDGE = 5
SLOT = 4
LANES = 128
SIB, EVEN, ODD, CROSS = range(4)


def orient_tables(edge_nodes, components):
    node_ids = np.arange(edge_nodes * edge_nodes)
    row_pos = node_ids // edge_nodes
    col_pos = node_ids % edge_nodes
    table_rows = []
    for orient_code in range(8):
        if orient_code & 4:
            first_pos, second_pos = (col_pos, row_pos)
        else:
            first_pos, second_pos = (row_pos, col_pos)
        if orient_code & 1:
            first_pos = edge_nodes - 1 - first_pos
        if orient_code & 2:
            second_pos = edge_nodes - 1 - second_pos
        moved_node = first_pos * edge_nodes + second_pos
        table_rows.append(
            np.concatenate(
                [
                    part_index * edge_nodes * edge_nodes + moved_node
                    for part_index in range(components)
                ]
            )
        )
    forward = np.stack(table_rows).astype(np.int32)
    backward = np.argsort(forward, axis=1).astype(np.int32)
    return (forward, backward)


def window_rows(trace_len):
    dof = 6 * trace_len
    for height in range(trace_len, dof):
        last = dof - height
        starts = [min(trace_len * k // 16 * 16, last) for k in range(6)]
        if last % 16 == 0 and all(
            start + height >= trace_len * (k + 1) for k, start in enumerate(starts)
        ):
            return height, last
    return dof, 0


def lane_tables(trace_len):
    forward, backward = orient_tables(EDGE, COMP)
    gap = LANES - trace_len
    spare = np.arange(trace_len, LANES)
    lanes = np.arange(LANES)
    _, last = window_rows(trace_len)
    into = np.zeros((6 * 8, LANES), np.int32)
    window = np.zeros((6 * 8, LANES), np.int32)
    outof = np.zeros((6 * 8, LANES), np.int32)
    for k in range(6):
        start = min(trace_len * k // 16 * 16, last)
        for code in range(8):
            full = np.concatenate([forward[code], spare])
            into[k * 8 + code] = full[(lanes + gap * k) % LANES]
            window[k * 8 + code] = full[(lanes - (trace_len * k - start)) % LANES]
            full = np.concatenate([backward[code], spare])
            outof[k * 8 + code] = (full - gap * k) % LANES
    return np.stack([into, window, outof])


def swap_routes(devices):
    routes = [[(i, i ^ 1) for i in range(devices)]]
    for shift in (0, 2):
        route = []
        for i in range(devices):
            other = ((i - shift) ^ 3) + shift
            route.append((i, other if i >= shift and other < devices else i ^ 1))
        routes.append(route)
    return routes


def partners(me):
    core = me & 1
    odd_chip = (me >> 1) & 1
    return (
        me ^ 1,
        me + 2 - 4 * odd_chip,
        me - 2 + 4 * odd_chip,
        me - 1 + 2 * core,
    )


def crossing_bucket(from_even, from_odd):
    me = lax.axis_index("elem")
    by_even = jnp.broadcast_to(((me ^ (me >> 1)) & 1) == 1, from_even.shape[1:])
    return [jnp.where(by_even, from_even[r], from_odd[r]) for r in range(SLOT)]


def put_bucket(group, r, tile, swap, even):
    target, first = {SIB: (swap, 0), ODD: (swap, SLOT), CROSS: (even, 0), EVEN: (even, SLOT)}[group]
    target[first + r] = tile


def start_all(pairs, sems):
    copies = [
        pltpu.make_async_copy(src, dst, sems.at[i]) for i, (src, dst) in enumerate(pairs)
    ]
    for copy in copies:
        copy.start()
    return copies


def permuted(tile, index):
    index = jnp.broadcast_to(index, tile.shape)
    return jnp.take_along_axis(tile, index, axis=1, mode="promise_in_bounds")


def lanes_from(array, start):
    width = 2 * LANES
    block = jnp.clip(start // LANES, 0, array.shape[1] // LANES - 2)
    window = array[:, pl.ds(pl.multiple_of(block * LANES, LANES), width)]
    shift = block * LANES - start
    window = jnp.concatenate([window, window[:2]])
    return pltpu.roll(window, jnp.where(shift < 0, shift + width, shift), 1)[:, :LANES]


def sum_before(counts, elem, elem_cap):
    elem = jnp.broadcast_to(elem, counts.shape)
    total = counts
    step = 1
    while step < elem_cap:
        total = total + jnp.where(elem >= step, pltpu.roll(total, step, 1), 0.0)
        step *= 2
    return total - counts


def wanted_faces(me, elem_cap, devices, face_dev, faces, counts):
    window = lanes_from(faces, (me - 2) * elem_cap)
    lane = lax.broadcasted_iota(jnp.int32, (1, LANES), 1)
    span = sum((lane >= elem_cap * q).astype(jnp.int32) for q in range(1, 6))
    elem = lane - elem_cap * span
    limit = jnp.zeros_like(lane)
    for q in (0, 1, 3, 4):
        device = me + q - 2
        inside = (device >= 0) & (device < devices)
        count = jnp.where(inside, counts[jnp.clip(device, 0, devices - 1)], 0)
        limit = jnp.where(span == q, count, limit)
    local = [(window[k : k + 1] - me * face_dev) for k in range(6)]
    hits = [(x >= 0) & (x < face_dev) & (elem < limit) for x in local]
    ones = [hit.astype(jnp.float32) for hit in hits]
    column = sum(ones)
    rank = sum_before(jnp.broadcast_to(column, (8, LANES)), elem, elem_cap)[:1]
    found = [jnp.zeros((1, LANES), jnp.float32) for _ in range(SLOT)]
    for k in range(6):
        value = jnp.where(hits[k], local[k].astype(jnp.float32), 0.0)
        for r in range(SLOT):
            found[r] = found[r] + jnp.where(rank == r, value, 0.0)
        rank = rank + ones[k]
    slots = []
    for device in partners(me):
        inside = (device >= 0) & (device < devices)
        for r in range(SLOT):
            slot = jnp.sum(jnp.where(span == device - me + 2, found[r], 0.0)).astype(jnp.int32)
            slots.append(jnp.where(inside, slot, face_dev))
    return slots


def first_kernel(
    elem_cap,
    devices,
    faces_hbm,
    counts_hbm,
    rhs_hbm,
    blocks_hbm,
    traces,
    rounded,
    swap,
    even,
    slots,
    faces,
    counts,
    rhs,
    blocks,
    sems,
):
    me = lax.axis_index("elem")
    face_dev, functionals, trace_len = rhs.shape
    copies = start_all(
        [(faces_hbm, faces), (counts_hbm, counts), (rhs_hbm, rhs), (blocks_hbm, blocks)], sems
    )
    copies[0].wait()
    copies[1].wait()
    picked = wanted_faces(me, elem_cap, devices, face_dev, faces, counts)
    for i, slot in enumerate(picked):
        slots[i : i + 1, :] = jnp.full((1, LANES), slot)
    copies[2].wait()
    copies[3].wait()
    for f in range(face_dev):
        value = jnp.dot(rhs[f], blocks[f], preferred_element_type=jnp.float32)
        traces[f, :, :trace_len] = value
        rounded[f, :, :trace_len] = value.astype(jnp.bfloat16)
    for group in range(4):
        for r in range(SLOT):
            slot = picked[group * SLOT + r]
            tile = rounded[jnp.where(slot < face_dev, slot, 0)]
            put_bucket(group, r, tile, swap, even)


def own_lists(me, elem_cap, face_dev, faces, orient, counts):
    window = lanes_from(faces, me * elem_cap)
    codes = lanes_from(orient, me * elem_cap)
    lane = lax.broadcasted_iota(jnp.int32, (1, LANES), 1)
    every = lax.broadcasted_iota(jnp.int32, (1, counts.shape[0]), 1)
    count = jnp.sum(jnp.where(every == me, counts[...].reshape(every.shape), 0).astype(jnp.float32))
    used = lane.astype(jnp.float32) < count
    rel = [window[k : k + 1] - (me - 2) * face_dev for k in range(6)]
    owner = [sum((x >= face_dev * j).astype(jnp.int32) for j in range(1, 5)) for x in rel]
    owner = [jnp.where(used, x, 2) for x in owner]
    others = [0, 1, 3, 4]
    column = [sum((x == j).astype(jnp.float32) for x in owner) for j in others]
    column = jnp.concatenate(column + [jnp.zeros((4, LANES), jnp.float32)])
    ranks = sum_before(column, lane, elem_cap).astype(jnp.int32)
    heads = []
    for i, j in enumerate(others):
        base = sum(
            jnp.where(device == me + j - 2, group * SLOT, 0)
            for group, device in enumerate(partners(me))
        )
        heads.append(ranks[i : i + 1] + base)
    gather, home, slots, picks = [], [], [], []
    for k in range(6):
        slot = jnp.full_like(lane, 4 * SLOT)
        for i, j in enumerate(others):
            hit = owner[k] == j
            slot = jnp.where(hit, heads[i], slot)
            heads[i] = heads[i] + hit.astype(jnp.int32)
        place = jnp.where(used & (owner[k] == 2), rel[k] - 2 * face_dev, face_dev)
        gather.append(jnp.where(slot < SLOT, face_dev + 1 + slot, place))
        home.append(place)
        slots.append(slot)
        picks.append(codes[k : k + 1] + 8 * k)
    return gather, home, slots, picks


def rows_kernel(
    elem_cap,
    faces,
    orient,
    counts,
    tables,
    rounded,
    from_sib,
    rows,
    sums,
    remote,
    index_in,
    table,
):
    me = lax.axis_index("elem")
    face_dev, functionals, _ = rounded.shape
    live = rows.shape[0]
    trace_len = COMP * EDGE * EDGE
    gap = LANES - trace_len
    table[:face_dev] = rounded[...]
    table[face_dev] = jnp.zeros((functionals, LANES), jnp.bfloat16)
    table[face_dev + 1 :] = from_sib[:SLOT]
    gather, home, slots, picks = own_lists(me, elem_cap, face_dev, faces, orient, counts)
    packed = [gather[k] * 64 + picks[k] for k in range(6)]
    for k in range(6):
        sums[k : k + 1, :] = home[k] * 64 + picks[k]
    lane = lax.broadcasted_iota(jnp.int32, (functionals, LANES), 1)
    for e in range(live):
        parts = []
        for k in range(6):
            code = packed[k][0, e]
            tile = table[code >> 6].astype(jnp.float32)
            parts.append(permuted(tile, tables[0, pl.ds(code & 63, 1), :]))
        for k in range(6):
            later = parts[k + 1] if k < 5 else jnp.zeros_like(parts[k])
            merged = jnp.where(lane < trace_len - gap * k, parts[k], later)
            rows[e, :, k * LANES : (k + 1) * LANES] = merged.astype(jnp.bfloat16)
    elem = lax.broadcasted_iota(jnp.int32, (1, LANES), 1)
    for t in range(4 * SLOT):
        entry = jnp.zeros((1, LANES), jnp.float32)
        for k in range(6):
            code = ((elem - live) * 8 + k) * 64 + picks[k]
            entry = entry + jnp.where(slots[k] == t, code.astype(jnp.float32), 0.0)
        code = jnp.sum(entry).astype(jnp.int32) + live * 512
        remote[t : t + 1, :] = jnp.full((1, LANES), code)
        index_in[t : t + 1, :] = tables[1, pl.ds(code & 63, 1), :]


def home_kernel(rows, mats, terms):
    live = rows.shape[0]
    dof = mats.shape[1]
    for e in range(live):
        terms[e, :, :dof] = jnp.dot(rows[e, :, :dof], mats[e], preferred_element_type=jnp.float32)
    terms[live] = jnp.zeros(terms.shape[1:], jnp.float32)


def unpacked(packs, t):
    packed = packs[t, 0]
    return packed >> 9, (packed >> 6) & 7, packed & 63


def add_remote(group, arrived, first, packs, index_in, mats, terms):
    live = terms.shape[0] - 1
    trace_len = mats.shape[1] // 6
    gap = LANES - trace_len
    height, last = window_rows(trace_len)
    lane = lax.broadcasted_iota(jnp.int32, arrived[first].shape, 1)
    for r in range(SLOT):
        t = group * SLOT + r
        e, k, _ = unpacked(packs, t)
        start = jnp.minimum((trace_len * k) >> 4 << 4, last)
        shift = trace_len * k - start
        tile = permuted(arrived[first + r].astype(jnp.float32), index_in[t : t + 1, :])
        zero = jnp.zeros_like(tile)
        wide = jnp.concatenate(
            [
                jnp.where((lane >= shift) & (lane < shift + trace_len), tile, zero),
                jnp.where(lane < shift - gap, tile, zero),
            ],
            axis=1,
        ).astype(jnp.bfloat16)
        window = mats[jnp.minimum(e, live - 1), pl.ds(pl.multiple_of(start, 16), height), :]
        terms[e, :, : 6 * trace_len] += jnp.dot(
            wide[:, :height], window, preferred_element_type=jnp.float32
        )


def relay_kernel(from_even, _, out):
    out[...] = from_even[SLOT:]


def even_kernel(remote, index_in, relayed, mats, _, terms):
    add_remote(EVEN, relayed, 0, remote[...], index_in, mats, terms)


def remote_kernel(
    remote, index_in, tables, from_even, from_odd, mats, _, swap, even, terms
):
    trace_len = mats.shape[1] // 6
    gap = LANES - trace_len
    packs = remote[...]
    add_remote(CROSS, crossing_bucket(from_even, from_odd), 0, packs, index_in, mats, terms)
    add_remote(ODD, from_odd, SLOT, packs, index_in, mats, terms)
    lane = lax.broadcasted_iota(jnp.int32, from_odd.shape[1:], 1)
    for group in range(4):
        for r in range(SLOT):
            e, k, pick = unpacked(packs, group * SLOT + r)
            tile = terms[e, :, pl.ds(pl.multiple_of(k * LANES, LANES), LANES)]
            ahead = jnp.maximum(k - 1, 0)
            left = terms[e, :, pl.ds(pl.multiple_of(ahead * LANES, LANES), LANES)]
            tile = jnp.where(lane >= LANES - gap * k, left, tile)
            tile = permuted(tile, tables[2, pl.ds(pick, 1), :]).astype(jnp.bfloat16)
            put_bucket(group, r, tile, swap, even)


def scatter_kernel(sums, tables, terms, rhs, base):
    face_dev, functionals, trace_len = rhs.shape
    live = terms.shape[0] - 1
    gap = LANES - trace_len
    lane = lax.broadcasted_iota(jnp.int32, (functionals, LANES), 1)
    base[:face_dev, :, :trace_len] = rhs[...].astype(jnp.float32)
    base[face_dev] = jnp.zeros((functionals, LANES), jnp.float32)
    codes = sums[...]
    for e in range(live):
        for k in range(6):
            tile = terms[e, :, k * LANES : (k + 1) * LANES]
            if k:
                left = terms[e, :, (k - 1) * LANES : k * LANES]
                tile = jnp.where(lane >= LANES - gap * k, left, tile)
            code = codes[k, e]
            tile = permuted(tile, tables[2, pl.ds(code & 63, 1), :])
            place = code >> 6
            base[place] -= tile.astype(jnp.bfloat16).astype(jnp.float32)


def last_kernel(
    slots, base, from_sib, from_even, from_odd, relayed, blocks, traces, out, residual
):
    face_dev, _, trace_len = out.shape
    residual[...] = base[...]
    crossing = crossing_bucket(from_even, from_odd)
    places = slots[...]
    for r in range(SLOT):
        arrived = {SIB: from_sib[r], EVEN: relayed[r], ODD: from_odd[SLOT + r], CROSS: crossing[r]}
        for group, tile in arrived.items():
            place = places[group * SLOT + r, 0]
            residual[place] -= tile.astype(jnp.float32)
    for f in range(face_dev):
        update = jnp.dot(
            residual[f, :, :trace_len].astype(jnp.bfloat16),
            blocks[f],
            preferred_element_type=jnp.float32,
        )
        out[f] = traces[f, :, :trace_len] + update


def exchange(routes, swap, even):
    sibling, even_chips, odd_chips = routes
    from_even = lax.ppermute(even, "elem", even_chips)
    from_sib = lax.ppermute(swap, "elem", sibling)
    odd = jnp.concatenate([even[:SLOT], from_sib[SLOT:]])
    return from_sib, from_even, lax.ppermute(odd, "elem", odd_chips)


def per_device(devices, elem_mats, face_blocks, rhs, elem_faces, orient, counts):
    elem_cap, dof, _ = elem_mats.shape
    face_dev, functionals, trace_len = rhs.shape
    live = elem_cap - elem_cap // 4
    far = 4 * SLOT
    routes = swap_routes(devices)

    def in_hbm(array):
        return pltpu.with_memory_space_constraint(array, pltpu.HBM)

    def in_vmem(array):
        return pltpu.with_memory_space_constraint(array, pltpu.VMEM)

    faces = in_hbm(elem_faces.T)
    tables = jnp.asarray(lane_tables(trace_len))
    vmem = pl.BlockSpec(memory_space=pltpu.VMEM)
    smem = pl.BlockSpec(memory_space=pltpu.SMEM)
    hbm = pl.BlockSpec(memory_space=pltpu.HBM)

    def tiles(count, kind, width=LANES):
        return jax.ShapeDtypeStruct((count, functionals, width), kind)

    def integers(*shape):
        return jax.ShapeDtypeStruct(shape, jnp.int32)

    params = pltpu.CompilerParams(vmem_limit_bytes=4 << 20)
    counts_smem = pltpu.SMEM(counts.shape, jnp.int32)
    traces, rounded, swap, even, slots = pl.pallas_call(
        functools.partial(first_kernel, elem_cap, devices),
        out_shape=(
            tiles(face_dev, jnp.float32),
            tiles(face_dev, jnp.bfloat16),
            tiles(2 * SLOT, jnp.bfloat16),
            tiles(2 * SLOT, jnp.bfloat16),
            integers(far, LANES),
        ),
        in_specs=[hbm] * 4,
        out_specs=(vmem,) * 5,
        scratch_shapes=[
            pltpu.VMEM(faces.shape, jnp.int32),
            counts_smem,
            pltpu.VMEM(rhs.shape, rhs.dtype),
            pltpu.VMEM(face_blocks.shape, face_blocks.dtype),
            pltpu.SemaphoreType.DMA((4,)),
        ],
        compiler_params=params,
        cost_estimate=pl.CostEstimate(
            flops=10**11, bytes_accessed=10**8, transcendentals=0
        ),
        name="first_sweep",
    )(faces, in_hbm(counts), in_hbm(rhs), in_hbm(face_blocks))
    def passed_on(from_even, after):
        relay = pl.pallas_call(
            relay_kernel,
            out_shape=tiles(SLOT, jnp.bfloat16),
            in_specs=[vmem, pl.BlockSpec(memory_space=pl.ANY)],
            out_specs=vmem,
            compiler_params=params,
            name="relay",
        )(from_even, after)
        return lax.ppermute(relay, "elem", routes[0])

    from_sib, from_even, from_odd = exchange(routes, swap, even)
    all_terms = pltpu.VMEM((live + 1, functionals, 6 * LANES), jnp.float32)
    rows, sums, remote, index_in = pl.pallas_call(
        functools.partial(rows_kernel, elem_cap),
        out_shape=(
            tiles(live, jnp.bfloat16, 6 * LANES),
            integers(6, LANES),
            integers(far, LANES),
            integers(far, LANES),
        ),
        in_specs=[vmem] * 6,
        out_specs=(vmem,) * 4,
        scratch_shapes=[pltpu.VMEM((face_dev + 1 + SLOT, functionals, LANES), jnp.bfloat16)],
        compiler_params=params,
        name="home_rows",
    )(elem_faces.T, orient.T, counts, tables, rounded, from_sib)
    terms = pl.pallas_call(
        home_kernel,
        out_shape=all_terms,
        in_specs=[vmem] * 2,
        out_specs=vmem,
        compiler_params=params,
        cost_estimate=pl.CostEstimate(
            flops=2 * live * functionals * dof * dof,
            bytes_accessed=2 * live * dof * dof,
            transcendentals=0,
        ),
        name="home_terms",
    )(rows, in_vmem(elem_mats))
    relayed = passed_on(from_even, sums)
    terms = pl.pallas_call(
        even_kernel,
        out_shape=all_terms,
        in_specs=[vmem] * 5,
        out_specs=vmem,
        input_output_aliases={4: 0},
        compiler_params=params,
        name="even_terms",
    )(remote, index_in, relayed, in_vmem(elem_mats), in_vmem(terms))
    swap, even, terms = pl.pallas_call(
        remote_kernel,
        out_shape=(tiles(2 * SLOT, jnp.bfloat16), tiles(2 * SLOT, jnp.bfloat16), all_terms),
        in_specs=[vmem] * 7,
        out_specs=(vmem,) * 3,
        input_output_aliases={6: 2},
        compiler_params=params,
        name="remote_terms",
    )(
        remote,
        index_in,
        tables,
        from_even,
        from_odd,
        in_vmem(elem_mats),
        in_vmem(terms),
    )
    from_sib, from_even, from_odd = exchange(routes, swap, even)
    base = pl.pallas_call(
        scatter_kernel,
        out_shape=tiles(face_dev + 1, jnp.float32),
        in_specs=[vmem] * 4,
        out_specs=vmem,
        compiler_params=params,
        name="home_sum",
    )(sums, tables, terms, rhs)
    relayed = passed_on(from_even, base)
    return pl.pallas_call(
        last_kernel,
        out_shape=jax.ShapeDtypeStruct(rhs.shape, jnp.float32),
        in_specs=[vmem] * 8,
        out_specs=vmem,
        scratch_shapes=[
            pltpu.VMEM((face_dev + 1, functionals, LANES), jnp.float32),
        ],
        compiler_params=params,
        name="last_update",
    )(slots, base, from_sib, from_even, from_odd, relayed, face_blocks, traces)


def solution(mesh):
    in_specs = (P("elem", None, None), P("elem", None, None), P("elem", None, None), P(), P(), P())
    out_specs = P("elem", None, None)
    return jax.shard_map(
        functools.partial(per_device, mesh.shape["elem"]),
        mesh=mesh,
        in_specs=in_specs,
        out_specs=out_specs,
        check_vma=False,
    )
```

```python
import functools

import jax
import jax.numpy as jnp
import numpy as np
from jax import lax
from jax.experimental import pallas as pl
from jax.experimental.pallas import tpu as pltpu
from jax.sharding import PartitionSpec as P

COMP = 5
EDGE = 5
SLOT = 4
LANES = 128
SIB, EVEN, ODD, CROSS = range(4)


def orient_tables(edge_nodes, components):
    node_ids = np.arange(edge_nodes * edge_nodes)
    row_pos = node_ids // edge_nodes
    col_pos = node_ids % edge_nodes
    table_rows = []
    for orient_code in range(8):
        if orient_code & 4:
            first_pos, second_pos = (col_pos, row_pos)
        else:
            first_pos, second_pos = (row_pos, col_pos)
        if orient_code & 1:
            first_pos = edge_nodes - 1 - first_pos
        if orient_code & 2:
            second_pos = edge_nodes - 1 - second_pos
        moved_node = first_pos * edge_nodes + second_pos
        table_rows.append(
            np.concatenate(
                [
                    part_index * edge_nodes * edge_nodes + moved_node
                    for part_index in range(components)
                ]
            )
        )
    forward = np.stack(table_rows).astype(np.int32)
    backward = np.argsort(forward, axis=1).astype(np.int32)
    return (forward, backward)


def window_rows(trace_len):
    dof = 6 * trace_len
    for height in range(trace_len, dof):
        last = dof - height
        starts = [min(trace_len * k // 16 * 16, last) for k in range(6)]
        if last % 16 == 0 and all(
            start + height >= trace_len * (k + 1) for k, start in enumerate(starts)
        ):
            return height, last
    return dof, 0


def lane_tables(trace_len):
    forward, backward = orient_tables(EDGE, COMP)
    gap = LANES - trace_len
    spare = np.arange(trace_len, LANES)
    lanes = np.arange(LANES)
    _, last = window_rows(trace_len)
    into = np.zeros((6 * 8, LANES), np.int32)
    window = np.zeros((6 * 8, LANES), np.int32)
    outof = np.zeros((6 * 8, LANES), np.int32)
    for k in range(6):
        start = min(trace_len * k // 16 * 16, last)
        for code in range(8):
            full = np.concatenate([forward[code], spare])
            into[k * 8 + code] = full[(lanes + gap * k) % LANES]
            window[k * 8 + code] = full[(lanes - (trace_len * k - start)) % LANES]
            full = np.concatenate([backward[code], spare])
            outof[k * 8 + code] = (full - gap * k) % LANES
    return np.stack([into, window, outof])


def swap_routes(devices):
    routes = [[(i, i ^ 1) for i in range(devices)]]
    for shift in (0, 2):
        route = []
        for i in range(devices):
            other = ((i - shift) ^ 3) + shift
            route.append((i, other if i >= shift and other < devices else i ^ 1))
        routes.append(route)
    return routes


def partners(me):
    core = me & 1
    odd_chip = (me >> 1) & 1
    return (
        me ^ 1,
        me + 2 - 4 * odd_chip,
        me - 2 + 4 * odd_chip,
        me - 1 + 2 * core,
    )


def crossing_bucket(from_even, from_odd):
    me = lax.axis_index("elem")
    by_even = jnp.broadcast_to(((me ^ (me >> 1)) & 1) == 1, from_even.shape[1:])
    return [jnp.where(by_even, from_even[r], from_odd[r]) for r in range(SLOT)]


def put_bucket(group, r, tile, swap, even):
    target, first = {SIB: (swap, 0), ODD: (swap, SLOT), CROSS: (even, 0), EVEN: (even, SLOT)}[group]
    target[first + r] = tile


def start_all(pairs, sems):
    copies = [
        pltpu.make_async_copy(src, dst, sems.at[i]) for i, (src, dst) in enumerate(pairs)
    ]
    for copy in copies:
        copy.start()
    return copies


def permuted(tile, index):
    index = jnp.broadcast_to(index, tile.shape)
    return jnp.take_along_axis(tile, index, axis=1, mode="promise_in_bounds")


def lanes_from(array, start):
    width = 2 * LANES
    block = jnp.clip(start // LANES, 0, array.shape[1] // LANES - 2)
    window = array[:, pl.ds(pl.multiple_of(block * LANES, LANES), width)]
    shift = block * LANES - start
    window = jnp.concatenate([window, window[:2]])
    return pltpu.roll(window, jnp.where(shift < 0, shift + width, shift), 1)[:, :LANES]


def sum_before(counts, elem, elem_cap):
    elem = jnp.broadcast_to(elem, counts.shape)
    total = counts
    step = 1
    while step < elem_cap:
        total = total + jnp.where(elem >= step, pltpu.roll(total, step, 1), 0.0)
        step *= 2
    return total - counts


def wanted_faces(me, elem_cap, devices, face_dev, faces, counts):
    window = lanes_from(faces, (me - 2) * elem_cap)
    lane = lax.broadcasted_iota(jnp.int32, (1, LANES), 1)
    span = sum((lane >= elem_cap * q).astype(jnp.int32) for q in range(1, 6))
    elem = lane - elem_cap * span
    limit = jnp.zeros_like(lane)
    for q in (0, 1, 3, 4):
        device = me + q - 2
        inside = (device >= 0) & (device < devices)
        count = jnp.where(inside, counts[jnp.clip(device, 0, devices - 1)], 0)
        limit = jnp.where(span == q, count, limit)
    local = [(window[k : k + 1] - me * face_dev) for k in range(6)]
    hits = [(x >= 0) & (x < face_dev) & (elem < limit) for x in local]
    ones = [hit.astype(jnp.float32) for hit in hits]
    column = sum(ones)
    rank = sum_before(jnp.broadcast_to(column, (8, LANES)), elem, elem_cap)[:1]
    found = [jnp.zeros((1, LANES), jnp.float32) for _ in range(SLOT)]
    for k in range(6):
        value = jnp.where(hits[k], local[k].astype(jnp.float32), 0.0)
        for r in range(SLOT):
            found[r] = found[r] + jnp.where(rank == r, value, 0.0)
        rank = rank + ones[k]
    slots = []
    for device in partners(me):
        inside = (device >= 0) & (device < devices)
        for r in range(SLOT):
            slot = jnp.sum(jnp.where(span == device - me + 2, found[r], 0.0)).astype(jnp.int32)
            slots.append(jnp.where(inside, slot, face_dev))
    return slots


def first_kernel(
    elem_cap,
    devices,
    faces_hbm,
    counts_hbm,
    rhs_hbm,
    blocks_hbm,
    traces,
    rounded,
    swap,
    even,
    slots,
    faces,
    counts,
    rhs,
    blocks,
    sems,
):
    me = lax.axis_index("elem")
    face_dev, functionals, trace_len = rhs.shape
    copies = start_all(
        [(faces_hbm, faces), (counts_hbm, counts), (rhs_hbm, rhs), (blocks_hbm, blocks)], sems
    )
    copies[0].wait()
    copies[1].wait()
    picked = wanted_faces(me, elem_cap, devices, face_dev, faces, counts)
    for i, slot in enumerate(picked):
        slots[i : i + 1, :] = jnp.full((1, LANES), slot)
    copies[2].wait()
    copies[3].wait()
    for f in range(face_dev):
        value = jnp.dot(rhs[f], blocks[f], preferred_element_type=jnp.float32)
        traces[f, :, :trace_len] = value
        rounded[f, :, :trace_len] = value.astype(jnp.bfloat16)
    for group in range(4):
        for r in range(SLOT):
            slot = picked[group * SLOT + r]
            tile = rounded[jnp.where(slot < face_dev, slot, 0)]
            put_bucket(group, r, tile, swap, even)


def own_lists(me, elem_cap, face_dev, faces, orient, counts):
    window = lanes_from(faces, me * elem_cap)
    codes = lanes_from(orient, me * elem_cap)
    lane = lax.broadcasted_iota(jnp.int32, (1, LANES), 1)
    every = lax.broadcasted_iota(jnp.int32, (1, counts.shape[0]), 1)
    count = jnp.sum(jnp.where(every == me, counts[...].reshape(every.shape), 0).astype(jnp.float32))
    used = lane.astype(jnp.float32) < count
    rel = [window[k : k + 1] - (me - 2) * face_dev for k in range(6)]
    owner = [sum((x >= face_dev * j).astype(jnp.int32) for j in range(1, 5)) for x in rel]
    owner = [jnp.where(used, x, 2) for x in owner]
    others = [0, 1, 3, 4]
    column = [sum((x == j).astype(jnp.float32) for x in owner) for j in others]
    column = jnp.concatenate(column + [jnp.zeros((4, LANES), jnp.float32)])
    ranks = sum_before(column, lane, elem_cap).astype(jnp.int32)
    heads = []
    for i, j in enumerate(others):
        base = sum(
            jnp.where(device == me + j - 2, group * SLOT, 0)
            for group, device in enumerate(partners(me))
        )
        heads.append(ranks[i : i + 1] + base)
    gather, home, slots, picks = [], [], [], []
    for k in range(6):
        slot = jnp.full_like(lane, 4 * SLOT)
        for i, j in enumerate(others):
            hit = owner[k] == j
            slot = jnp.where(hit, heads[i], slot)
            heads[i] = heads[i] + hit.astype(jnp.int32)
        place = jnp.where(used & (owner[k] == 2), rel[k] - 2 * face_dev, face_dev)
        gather.append(jnp.where(slot < SLOT, face_dev + 1 + slot, place))
        home.append(place)
        slots.append(slot)
        picks.append(codes[k : k + 1] + 8 * k)
    return gather, home, slots, picks


def rows_kernel(
    elem_cap,
    faces,
    orient,
    counts,
    tables,
    rounded,
    from_sib,
    rows,
    sums,
    remote,
    index_in,
    table,
):
    me = lax.axis_index("elem")
    face_dev, functionals, _ = rounded.shape
    live = rows.shape[0]
    trace_len = COMP * EDGE * EDGE
    gap = LANES - trace_len
    table[:face_dev] = rounded[...]
    table[face_dev] = jnp.zeros((functionals, LANES), jnp.bfloat16)
    table[face_dev + 1 :] = from_sib[:SLOT]
    gather, home, slots, picks = own_lists(me, elem_cap, face_dev, faces, orient, counts)
    packed = [gather[k] * 64 + picks[k] for k in range(6)]
    for k in range(6):
        sums[k : k + 1, :] = home[k] * 64 + picks[k]
    lane = lax.broadcasted_iota(jnp.int32, (functionals, LANES), 1)
    for e in range(live):
        parts = []
        for k in range(6):
            code = packed[k][0, e]
            tile = table[code >> 6].astype(jnp.float32)
            parts.append(permuted(tile, tables[0, pl.ds(code & 63, 1), :]))
        for k in range(6):
            later = parts[k + 1] if k < 5 else jnp.zeros_like(parts[k])
            merged = jnp.where(lane < trace_len - gap * k, parts[k], later)
            rows[e, :, k * LANES : (k + 1) * LANES] = merged.astype(jnp.bfloat16)
    elem = lax.broadcasted_iota(jnp.int32, (1, LANES), 1)
    for t in range(4 * SLOT):
        entry = jnp.zeros((1, LANES), jnp.float32)
        for k in range(6):
            code = ((elem - live) * 8 + k) * 64 + picks[k]
            entry = entry + jnp.where(slots[k] == t, code.astype(jnp.float32), 0.0)
        code = jnp.sum(entry).astype(jnp.int32) + live * 512
        remote[t : t + 1, :] = jnp.full((1, LANES), code)
        index_in[t : t + 1, :] = tables[1, pl.ds(code & 63, 1), :]


def home_kernel(rows, mats, terms):
    live = rows.shape[0]
    dof = mats.shape[1]
    for e in range(live):
        terms[e, :, :dof] = jnp.dot(rows[e, :, :dof], mats[e], preferred_element_type=jnp.float32)
    terms[live] = jnp.zeros(terms.shape[1:], jnp.float32)


def unpacked(packs, t):
    packed = packs[t, 0]
    return packed >> 9, (packed >> 6) & 7, packed & 63


def add_remote(group, arrived, first, packs, index_in, mats, terms):
    live = terms.shape[0] - 1
    trace_len = mats.shape[1] // 6
    gap = LANES - trace_len
    height, last = window_rows(trace_len)
    lane = lax.broadcasted_iota(jnp.int32, arrived[first].shape, 1)
    for r in range(SLOT):
        t = group * SLOT + r
        e, k, _ = unpacked(packs, t)
        start = jnp.minimum((trace_len * k) >> 4 << 4, last)
        shift = trace_len * k - start
        tile = permuted(arrived[first + r].astype(jnp.float32), index_in[t : t + 1, :])
        zero = jnp.zeros_like(tile)
        wide = jnp.concatenate(
            [
                jnp.where((lane >= shift) & (lane < shift + trace_len), tile, zero),
                jnp.where(lane < shift - gap, tile, zero),
            ],
            axis=1,
        ).astype(jnp.bfloat16)
        window = mats[jnp.minimum(e, live - 1), pl.ds(pl.multiple_of(start, 16), height), :]
        terms[e, :, : 6 * trace_len] += jnp.dot(
            wide[:, :height], window, preferred_element_type=jnp.float32
        )


def relay_kernel(from_even, _, out):
    out[...] = from_even[SLOT:]


def even_kernel(remote, index_in, relayed, mats, _, terms):
    add_remote(EVEN, relayed, 0, remote[...], index_in, mats, terms)


def remote_kernel(
    remote, index_in, tables, from_even, from_odd, mats, _, swap, even, terms
):
    trace_len = mats.shape[1] // 6
    gap = LANES - trace_len
    packs = remote[...]
    add_remote(CROSS, crossing_bucket(from_even, from_odd), 0, packs, index_in, mats, terms)
    add_remote(ODD, from_odd, SLOT, packs, index_in, mats, terms)
    lane = lax.broadcasted_iota(jnp.int32, from_odd.shape[1:], 1)
    for group in range(4):
        for r in range(SLOT):
            e, k, pick = unpacked(packs, group * SLOT + r)
            tile = terms[e, :, pl.ds(pl.multiple_of(k * LANES, LANES), LANES)]
            ahead = jnp.maximum(k - 1, 0)
            left = terms[e, :, pl.ds(pl.multiple_of(ahead * LANES, LANES), LANES)]
            tile = jnp.where(lane >= LANES - gap * k, left, tile)
            tile = permuted(tile, tables[2, pl.ds(pick, 1), :]).astype(jnp.bfloat16)
            put_bucket(group, r, tile, swap, even)


def scatter_kernel(sums, tables, terms, rhs, base):
    face_dev, functionals, trace_len = rhs.shape
    live = terms.shape[0] - 1
    gap = LANES - trace_len
    lane = lax.broadcasted_iota(jnp.int32, (functionals, LANES), 1)
    base[:face_dev, :, :trace_len] = rhs[...].astype(jnp.float32)
    base[face_dev] = jnp.zeros((functionals, LANES), jnp.float32)
    codes = sums[...]
    for e in range(live):
        for k in range(6):
            tile = terms[e, :, k * LANES : (k + 1) * LANES]
            if k:
                left = terms[e, :, (k - 1) * LANES : k * LANES]
                tile = jnp.where(lane >= LANES - gap * k, left, tile)
            code = codes[k, e]
            tile = permuted(tile, tables[2, pl.ds(code & 63, 1), :])
            place = code >> 6
            base[place] -= tile.astype(jnp.bfloat16).astype(jnp.float32)


def updated(residual, block, trace):
    trace_len = block.shape[0]
    update = jnp.dot(
        residual[:, :trace_len].astype(jnp.bfloat16), block, preferred_element_type=jnp.float32
    )
    return trace[:, :trace_len] + update


def crossing_part(arrived, by_even):
    me = lax.axis_index("elem")
    here = (((me ^ (me >> 1)) & 1) == 1) == by_even
    here = jnp.broadcast_to(here, arrived.shape[1:])
    return [jnp.where(here, arrived[r].astype(jnp.float32), 0.0) for r in range(SLOT)]


def early_kernel(slots, base, from_sib, from_even, relayed, blocks, traces, residual, early):
    face_dev = early.shape[0]
    residual[...] = base[...]
    crossing = crossing_part(from_even, True)
    places = slots[...]
    for r in range(SLOT):
        arrived = {SIB: from_sib[r], EVEN: relayed[r], CROSS: crossing[r]}
        for group, tile in arrived.items():
            place = places[group * SLOT + r, 0]
            residual[place] -= tile.astype(jnp.float32)
    for f in range(face_dev):
        early[f] = updated(residual[f], blocks[f], traces[f])


def last_kernel(slots, before, early, from_odd, blocks, traces, out, residual):
    face_dev = out.shape[0]
    residual[...] = before[...]
    out[...] = early[...]
    crossing = crossing_part(from_odd, False)
    codes = slots[...]
    places = {(g, r): codes[g * SLOT + r, 0] for g in (ODD, CROSS) for r in range(SLOT)}
    for (group, r), place in places.items():
        tile = crossing[r] if group == CROSS else from_odd[SLOT + r].astype(jnp.float32)
        residual[place] -= tile
    for place in places.values():
        f = jnp.minimum(place, face_dev - 1)
        out[f] = updated(residual[f], blocks[f], traces[f])


def exchange(routes, swap, even):
    sibling, even_chips, odd_chips = routes
    from_even = lax.ppermute(even, "elem", even_chips)
    from_sib = lax.ppermute(swap, "elem", sibling)
    odd = jnp.concatenate([even[:SLOT], from_sib[SLOT:]])
    return from_sib, from_even, lax.ppermute(odd, "elem", odd_chips)


def per_device(devices, elem_mats, face_blocks, rhs, elem_faces, orient, counts):
    elem_cap, dof, _ = elem_mats.shape
    face_dev, functionals, trace_len = rhs.shape
    live = elem_cap - elem_cap // 4
    far = 4 * SLOT
    routes = swap_routes(devices)

    def in_hbm(array):
        return pltpu.with_memory_space_constraint(array, pltpu.HBM)

    def in_vmem(array):
        return pltpu.with_memory_space_constraint(array, pltpu.VMEM)

    faces = in_hbm(elem_faces.T)
    tables = jnp.asarray(lane_tables(trace_len))
    vmem = pl.BlockSpec(memory_space=pltpu.VMEM)
    smem = pl.BlockSpec(memory_space=pltpu.SMEM)
    hbm = pl.BlockSpec(memory_space=pltpu.HBM)

    def tiles(count, kind, width=LANES):
        return jax.ShapeDtypeStruct((count, functionals, width), kind)

    def integers(*shape):
        return jax.ShapeDtypeStruct(shape, jnp.int32)

    params = pltpu.CompilerParams(vmem_limit_bytes=4 << 20)
    counts_smem = pltpu.SMEM(counts.shape, jnp.int32)
    traces, rounded, swap, even, slots = pl.pallas_call(
        functools.partial(first_kernel, elem_cap, devices),
        out_shape=(
            tiles(face_dev, jnp.float32),
            tiles(face_dev, jnp.bfloat16),
            tiles(2 * SLOT, jnp.bfloat16),
            tiles(2 * SLOT, jnp.bfloat16),
            integers(far, LANES),
        ),
        in_specs=[hbm] * 4,
        out_specs=(vmem,) * 5,
        scratch_shapes=[
            pltpu.VMEM(faces.shape, jnp.int32),
            counts_smem,
            pltpu.VMEM(rhs.shape, rhs.dtype),
            pltpu.VMEM(face_blocks.shape, face_blocks.dtype),
            pltpu.SemaphoreType.DMA((4,)),
        ],
        compiler_params=params,
        cost_estimate=pl.CostEstimate(
            flops=10**11, bytes_accessed=10**8, transcendentals=0
        ),
        name="first_sweep",
    )(faces, in_hbm(counts), in_hbm(rhs), in_hbm(face_blocks))
    def passed_on(from_even, after):
        relay = pl.pallas_call(
            relay_kernel,
            out_shape=tiles(SLOT, jnp.bfloat16),
            in_specs=[vmem, pl.BlockSpec(memory_space=pl.ANY)],
            out_specs=vmem,
            compiler_params=params,
            name="relay",
        )(from_even, after)
        return lax.ppermute(relay, "elem", routes[0])

    from_sib, from_even, from_odd = exchange(routes, swap, even)
    all_terms = pltpu.VMEM((live + 1, functionals, 6 * LANES), jnp.float32)
    rows, sums, remote, index_in = pl.pallas_call(
        functools.partial(rows_kernel, elem_cap),
        out_shape=(
            tiles(live, jnp.bfloat16, 6 * LANES),
            integers(6, LANES),
            integers(far, LANES),
            integers(far, LANES),
        ),
        in_specs=[vmem] * 6,
        out_specs=(vmem,) * 4,
        scratch_shapes=[pltpu.VMEM((face_dev + 1 + SLOT, functionals, LANES), jnp.bfloat16)],
        compiler_params=params,
        name="home_rows",
    )(elem_faces.T, orient.T, counts, tables, rounded, from_sib)
    terms = pl.pallas_call(
        home_kernel,
        out_shape=all_terms,
        in_specs=[vmem] * 2,
        out_specs=vmem,
        compiler_params=params,
        cost_estimate=pl.CostEstimate(
            flops=2 * live * functionals * dof * dof,
            bytes_accessed=2 * live * dof * dof,
            transcendentals=0,
        ),
        name="home_terms",
    )(rows, in_vmem(elem_mats))
    relayed = passed_on(from_even, sums)
    terms = pl.pallas_call(
        even_kernel,
        out_shape=all_terms,
        in_specs=[vmem] * 5,
        out_specs=vmem,
        input_output_aliases={4: 0},
        compiler_params=params,
        name="even_terms",
    )(remote, index_in, relayed, in_vmem(elem_mats), in_vmem(terms))
    swap, even, terms = pl.pallas_call(
        remote_kernel,
        out_shape=(tiles(2 * SLOT, jnp.bfloat16), tiles(2 * SLOT, jnp.bfloat16), all_terms),
        in_specs=[vmem] * 7,
        out_specs=(vmem,) * 3,
        input_output_aliases={6: 2},
        compiler_params=params,
        name="remote_terms",
    )(
        remote,
        index_in,
        tables,
        from_even,
        from_odd,
        in_vmem(elem_mats),
        in_vmem(terms),
    )
    from_sib, from_even, from_odd = exchange(routes, swap, even)
    base = pl.pallas_call(
        scatter_kernel,
        out_shape=tiles(face_dev + 1, jnp.float32),
        in_specs=[vmem] * 4,
        out_specs=vmem,
        compiler_params=params,
        name="home_sum",
    )(sums, tables, terms, rhs)
    relayed = passed_on(from_even, base)
    residual, early = pl.pallas_call(
        early_kernel,
        out_shape=(
            tiles(face_dev + 1, jnp.float32),
            jax.ShapeDtypeStruct(rhs.shape, jnp.float32),
        ),
        in_specs=[vmem] * 7,
        out_specs=(vmem,) * 2,
        compiler_params=params,
        name="early_update",
    )(slots, base, from_sib, from_even, relayed, face_blocks, traces)
    return pl.pallas_call(
        last_kernel,
        out_shape=jax.ShapeDtypeStruct(rhs.shape, jnp.float32),
        in_specs=[vmem] * 6,
        out_specs=vmem,
        scratch_shapes=[pltpu.VMEM((face_dev + 1, functionals, LANES), jnp.float32)],
        compiler_params=params,
        name="last_update",
    )(slots, residual, early, from_odd, face_blocks, traces)


def solution(mesh):
    in_specs = (P("elem", None, None), P("elem", None, None), P("elem", None, None), P(), P(), P())
    out_specs = P("elem", None, None)
    return jax.shard_map(
        functools.partial(per_device, mesh.shape["elem"]),
        mesh=mesh,
        in_specs=in_specs,
        out_specs=out_specs,
        check_vma=False,
    )
```

```python
import functools

import jax
import jax.numpy as jnp
import numpy as np
from jax import lax
from jax.experimental import pallas as pl
from jax.experimental.pallas import tpu as pltpu
from jax.sharding import PartitionSpec as P

COMP = 5
EDGE = 5
SLOT = 4
LANES = 128
SIB, EVEN, ODD, CROSS = range(4)


def orient_tables(edge_nodes, components):
    node_ids = np.arange(edge_nodes * edge_nodes)
    row_pos = node_ids // edge_nodes
    col_pos = node_ids % edge_nodes
    table_rows = []
    for orient_code in range(8):
        if orient_code & 4:
            first_pos, second_pos = (col_pos, row_pos)
        else:
            first_pos, second_pos = (row_pos, col_pos)
        if orient_code & 1:
            first_pos = edge_nodes - 1 - first_pos
        if orient_code & 2:
            second_pos = edge_nodes - 1 - second_pos
        moved_node = first_pos * edge_nodes + second_pos
        table_rows.append(
            np.concatenate(
                [
                    part_index * edge_nodes * edge_nodes + moved_node
                    for part_index in range(components)
                ]
            )
        )
    forward = np.stack(table_rows).astype(np.int32)
    backward = np.argsort(forward, axis=1).astype(np.int32)
    return (forward, backward)


def window_rows(trace_len):
    dof = 6 * trace_len
    for height in range(trace_len, dof):
        last = dof - height
        starts = [min(trace_len * k // 16 * 16, last) for k in range(6)]
        if last % 16 == 0 and all(
            start + height >= trace_len * (k + 1) for k, start in enumerate(starts)
        ):
            return height, last
    return dof, 0


def lane_tables(trace_len):
    forward, backward = orient_tables(EDGE, COMP)
    gap = LANES - trace_len
    spare = np.arange(trace_len, LANES)
    lanes = np.arange(LANES)
    _, last = window_rows(trace_len)
    into = np.zeros((6 * 8, LANES), np.int32)
    window = np.zeros((6 * 8, LANES), np.int32)
    outof = np.zeros((6 * 8, LANES), np.int32)
    for k in range(6):
        start = min(trace_len * k // 16 * 16, last)
        for code in range(8):
            full = np.concatenate([forward[code], spare])
            into[k * 8 + code] = full[(lanes + gap * k) % LANES]
            window[k * 8 + code] = full[(lanes - (trace_len * k - start)) % LANES]
            full = np.concatenate([backward[code], spare])
            outof[k * 8 + code] = (full - gap * k) % LANES
    return np.stack([into, window, outof])


def swap_routes(devices):
    routes = [[(i, i ^ 1) for i in range(devices)]]
    for shift in (0, 2):
        route = []
        for i in range(devices):
            other = ((i - shift) ^ 3) + shift
            route.append((i, other if i >= shift and other < devices else i ^ 1))
        routes.append(route)
    return routes


def partners(me):
    core = me & 1
    odd_chip = (me >> 1) & 1
    return (
        me ^ 1,
        me + 2 - 4 * odd_chip,
        me - 2 + 4 * odd_chip,
        me - 1 + 2 * core,
    )


def crossing_bucket(from_even, from_odd):
    me = lax.axis_index("elem")
    by_even = jnp.broadcast_to(((me ^ (me >> 1)) & 1) == 1, from_even.shape[1:])
    return [jnp.where(by_even, from_even[r], from_odd[r]) for r in range(SLOT)]


def put_bucket(group, r, tile, swap, even):
    target, first = {SIB: (swap, 0), ODD: (swap, SLOT), CROSS: (even, 0), EVEN: (even, SLOT)}[group]
    target[first + r] = tile


def start_all(pairs, sems):
    copies = [
        pltpu.make_async_copy(src, dst, sems.at[i]) for i, (src, dst) in enumerate(pairs)
    ]
    for copy in copies:
        copy.start()
    return copies


def permuted(tile, index):
    index = jnp.broadcast_to(index, tile.shape)
    return jnp.take_along_axis(tile, index, axis=1, mode="promise_in_bounds")


def lanes_from(array, start):
    width = 2 * LANES
    block = jnp.clip(start // LANES, 0, array.shape[1] // LANES - 2)
    window = array[:, pl.ds(pl.multiple_of(block * LANES, LANES), width)]
    shift = block * LANES - start
    window = jnp.concatenate([window, window[:2]])
    return pltpu.roll(window, jnp.where(shift < 0, shift + width, shift), 1)[:, :LANES]


def sum_before(counts, elem, elem_cap):
    elem = jnp.broadcast_to(elem, counts.shape)
    total = counts
    step = 1
    while step < elem_cap:
        total = total + jnp.where(elem >= step, pltpu.roll(total, step, 1), 0.0)
        step *= 2
    return total - counts


def wanted_faces(me, elem_cap, devices, face_dev, faces, counts):
    window = lanes_from(faces, (me - 2) * elem_cap)
    lane = lax.broadcasted_iota(jnp.int32, (1, LANES), 1)
    span = sum((lane >= elem_cap * q).astype(jnp.int32) for q in range(1, 6))
    elem = lane - elem_cap * span
    limit = jnp.zeros_like(lane)
    for q in (0, 1, 3, 4):
        device = me + q - 2
        inside = (device >= 0) & (device < devices)
        count = jnp.where(inside, counts[jnp.clip(device, 0, devices - 1)], 0)
        limit = jnp.where(span == q, count, limit)
    local = [(window[k : k + 1] - me * face_dev) for k in range(6)]
    hits = [(x >= 0) & (x < face_dev) & (elem < limit) for x in local]
    ones = [hit.astype(jnp.float32) for hit in hits]
    column = sum(ones)
    rank = sum_before(jnp.broadcast_to(column, (8, LANES)), elem, elem_cap)[:1]
    found = [jnp.zeros((1, LANES), jnp.float32) for _ in range(SLOT)]
    for k in range(6):
        value = jnp.where(hits[k], local[k].astype(jnp.float32), 0.0)
        for r in range(SLOT):
            found[r] = found[r] + jnp.where(rank == r, value, 0.0)
        rank = rank + ones[k]
    slots = []
    for device in partners(me):
        inside = (device >= 0) & (device < devices)
        for r in range(SLOT):
            slot = jnp.sum(jnp.where(span == device - me + 2, found[r], 0.0)).astype(jnp.int32)
            slots.append(jnp.where(inside, slot, face_dev))
    return slots


def first_traces(rhs, block):
    value = jnp.dot(rhs, block, preferred_element_type=jnp.float32)
    spare = jnp.zeros((value.shape[0], LANES - value.shape[1]), jnp.float32)
    return jnp.concatenate([value, spare], axis=1)


def traces_kernel(rhs, blocks, traces, rounded):
    for f in range(rhs.shape[0]):
        value = first_traces(rhs[f], blocks[f])
        traces[f] = value
        rounded[f] = value.astype(jnp.bfloat16)


def first_kernel(
    elem_cap,
    devices,
    faces_hbm,
    counts_hbm,
    rhs_hbm,
    blocks_hbm,
    swap,
    even,
    slots,
    faces,
    counts,
    rhs,
    blocks,
    sems,
):
    me = lax.axis_index("elem")
    face_dev = rhs.shape[0]
    copies = start_all(
        [(faces_hbm, faces), (counts_hbm, counts), (rhs_hbm, rhs), (blocks_hbm, blocks)], sems
    )
    copies[0].wait()
    copies[1].wait()
    picked = wanted_faces(me, elem_cap, devices, face_dev, faces, counts)
    for i, slot in enumerate(picked):
        slots[i : i + 1, :] = jnp.full((1, LANES), slot)
    copies[2].wait()
    copies[3].wait()
    for group in range(4):
        for r in range(SLOT):
            f = jnp.minimum(picked[group * SLOT + r], face_dev - 1)
            tile = first_traces(rhs[f], blocks[f]).astype(jnp.bfloat16)
            put_bucket(group, r, tile, swap, even)


def own_lists(me, elem_cap, face_dev, faces, orient, counts):
    window = lanes_from(faces, me * elem_cap)
    codes = lanes_from(orient, me * elem_cap)
    lane = lax.broadcasted_iota(jnp.int32, (1, LANES), 1)
    every = lax.broadcasted_iota(jnp.int32, (1, counts.shape[0]), 1)
    count = jnp.sum(jnp.where(every == me, counts[...].reshape(every.shape), 0).astype(jnp.float32))
    used = lane.astype(jnp.float32) < count
    rel = [window[k : k + 1] - (me - 2) * face_dev for k in range(6)]
    owner = [sum((x >= face_dev * j).astype(jnp.int32) for j in range(1, 5)) for x in rel]
    owner = [jnp.where(used, x, 2) for x in owner]
    others = [0, 1, 3, 4]
    column = [sum((x == j).astype(jnp.float32) for x in owner) for j in others]
    column = jnp.concatenate(column + [jnp.zeros((4, LANES), jnp.float32)])
    ranks = sum_before(column, lane, elem_cap).astype(jnp.int32)
    heads = []
    for i, j in enumerate(others):
        base = sum(
            jnp.where(device == me + j - 2, group * SLOT, 0)
            for group, device in enumerate(partners(me))
        )
        heads.append(ranks[i : i + 1] + base)
    gather, home, slots, picks = [], [], [], []
    for k in range(6):
        slot = jnp.full_like(lane, 4 * SLOT)
        for i, j in enumerate(others):
            hit = owner[k] == j
            slot = jnp.where(hit, heads[i], slot)
            heads[i] = heads[i] + hit.astype(jnp.int32)
        place = jnp.where(used & (owner[k] == 2), rel[k] - 2 * face_dev, face_dev)
        gather.append(jnp.where(slot < SLOT, face_dev + 1 + slot, place))
        home.append(place)
        slots.append(slot)
        picks.append(codes[k : k + 1] + 8 * k)
    return gather, home, slots, picks


def rows_kernel(
    elem_cap,
    faces,
    orient,
    counts,
    tables,
    rounded,
    from_sib,
    rows,
    sums,
    remote,
    index_in,
    table,
):
    me = lax.axis_index("elem")
    face_dev, functionals, _ = rounded.shape
    live = rows.shape[0]
    trace_len = COMP * EDGE * EDGE
    gap = LANES - trace_len
    table[:face_dev] = rounded[...]
    table[face_dev] = jnp.zeros((functionals, LANES), jnp.bfloat16)
    table[face_dev + 1 :] = from_sib[:SLOT]
    gather, home, slots, picks = own_lists(me, elem_cap, face_dev, faces, orient, counts)
    packed = [gather[k] * 64 + picks[k] for k in range(6)]
    for k in range(6):
        sums[k : k + 1, :] = home[k] * 64 + picks[k]
    lane = lax.broadcasted_iota(jnp.int32, (functionals, LANES), 1)
    for e in range(live):
        parts = []
        for k in range(6):
            code = packed[k][0, e]
            tile = table[code >> 6].astype(jnp.float32)
            parts.append(permuted(tile, tables[0, pl.ds(code & 63, 1), :]))
        for k in range(6):
            later = parts[k + 1] if k < 5 else jnp.zeros_like(parts[k])
            merged = jnp.where(lane < trace_len - gap * k, parts[k], later)
            rows[e, :, k * LANES : (k + 1) * LANES] = merged.astype(jnp.bfloat16)
    elem = lax.broadcasted_iota(jnp.int32, (1, LANES), 1)
    for t in range(4 * SLOT):
        entry = jnp.zeros((1, LANES), jnp.float32)
        for k in range(6):
            code = ((elem - live) * 8 + k) * 64 + picks[k]
            entry = entry + jnp.where(slots[k] == t, code.astype(jnp.float32), 0.0)
        code = jnp.sum(entry).astype(jnp.int32) + live * 512
        remote[t : t + 1, :] = jnp.full((1, LANES), code)
        index_in[t : t + 1, :] = tables[1, pl.ds(code & 63, 1), :]


def home_kernel(rows, mats, terms):
    live = rows.shape[0]
    dof = mats.shape[1]
    for e in range(live):
        terms[e, :, :dof] = jnp.dot(rows[e, :, :dof], mats[e], preferred_element_type=jnp.float32)
    terms[live] = jnp.zeros(terms.shape[1:], jnp.float32)


def unpacked(packs, t):
    packed = packs[t, 0]
    return packed >> 9, (packed >> 6) & 7, packed & 63


def add_remote(group, arrived, first, packs, index_in, mats, terms):
    live = terms.shape[0] - 1
    trace_len = mats.shape[1] // 6
    gap = LANES - trace_len
    height, last = window_rows(trace_len)
    lane = lax.broadcasted_iota(jnp.int32, arrived[first].shape, 1)
    for r in range(SLOT):
        t = group * SLOT + r
        e, k, _ = unpacked(packs, t)
        start = jnp.minimum((trace_len * k) >> 4 << 4, last)
        shift = trace_len * k - start
        tile = permuted(arrived[first + r].astype(jnp.float32), index_in[t : t + 1, :])
        zero = jnp.zeros_like(tile)
        wide = jnp.concatenate(
            [
                jnp.where((lane >= shift) & (lane < shift + trace_len), tile, zero),
                jnp.where(lane < shift - gap, tile, zero),
            ],
            axis=1,
        ).astype(jnp.bfloat16)
        window = mats[jnp.minimum(e, live - 1), pl.ds(pl.multiple_of(start, 16), height), :]
        terms[e, :, : 6 * trace_len] += jnp.dot(
            wide[:, :height], window, preferred_element_type=jnp.float32
        )


def relay_kernel(from_even, _, out):
    out[...] = from_even[SLOT:]


def even_kernel(remote, index_in, relayed, mats, _, terms):
    add_remote(EVEN, relayed, 0, remote[...], index_in, mats, terms)


def remote_kernel(
    remote, index_in, tables, from_even, from_odd, mats, _, swap, even, terms
):
    trace_len = mats.shape[1] // 6
    gap = LANES - trace_len
    packs = remote[...]
    add_remote(CROSS, crossing_bucket(from_even, from_odd), 0, packs, index_in, mats, terms)
    add_remote(ODD, from_odd, SLOT, packs, index_in, mats, terms)
    lane = lax.broadcasted_iota(jnp.int32, from_odd.shape[1:], 1)
    for group in range(4):
        for r in range(SLOT):
            e, k, pick = unpacked(packs, group * SLOT + r)
            tile = terms[e, :, pl.ds(pl.multiple_of(k * LANES, LANES), LANES)]
            ahead = jnp.maximum(k - 1, 0)
            left = terms[e, :, pl.ds(pl.multiple_of(ahead * LANES, LANES), LANES)]
            tile = jnp.where(lane >= LANES - gap * k, left, tile)
            tile = permuted(tile, tables[2, pl.ds(pick, 1), :]).astype(jnp.bfloat16)
            put_bucket(group, r, tile, swap, even)


def scatter_kernel(sums, tables, terms, rhs, base):
    face_dev, functionals, trace_len = rhs.shape
    live = terms.shape[0] - 1
    gap = LANES - trace_len
    lane = lax.broadcasted_iota(jnp.int32, (functionals, LANES), 1)
    base[:face_dev, :, :trace_len] = rhs[...].astype(jnp.float32)
    base[face_dev] = jnp.zeros((functionals, LANES), jnp.float32)
    codes = sums[...]
    for e in range(live):
        for k in range(6):
            tile = terms[e, :, k * LANES : (k + 1) * LANES]
            if k:
                left = terms[e, :, (k - 1) * LANES : k * LANES]
                tile = jnp.where(lane >= LANES - gap * k, left, tile)
            code = codes[k, e]
            tile = permuted(tile, tables[2, pl.ds(code & 63, 1), :])
            place = code >> 6
            base[place] -= tile.astype(jnp.bfloat16).astype(jnp.float32)


def updated(residual, block, trace):
    trace_len = block.shape[0]
    update = jnp.dot(
        residual[:, :trace_len].astype(jnp.bfloat16), block, preferred_element_type=jnp.float32
    )
    return trace[:, :trace_len] + update


def crossing_part(arrived, by_even):
    me = lax.axis_index("elem")
    here = (((me ^ (me >> 1)) & 1) == 1) == by_even
    here = jnp.broadcast_to(here, arrived.shape[1:])
    return [jnp.where(here, arrived[r].astype(jnp.float32), 0.0) for r in range(SLOT)]


def early_kernel(slots, base, from_sib, from_even, relayed, blocks, traces, residual, early):
    face_dev = early.shape[0]
    residual[...] = base[...]
    crossing = crossing_part(from_even, True)
    places = slots[...]
    for r in range(SLOT):
        arrived = {SIB: from_sib[r], EVEN: relayed[r], CROSS: crossing[r]}
        for group, tile in arrived.items():
            place = places[group * SLOT + r, 0]
            residual[place] -= tile.astype(jnp.float32)
    for f in range(face_dev):
        early[f] = updated(residual[f], blocks[f], traces[f])


def last_kernel(slots, before, early, from_odd, blocks, traces, out, residual):
    face_dev = out.shape[0]
    residual[...] = before[...]
    out[...] = early[...]
    crossing = crossing_part(from_odd, False)
    codes = slots[...]
    places = {(g, r): codes[g * SLOT + r, 0] for g in (ODD, CROSS) for r in range(SLOT)}
    for (group, r), place in places.items():
        tile = crossing[r] if group == CROSS else from_odd[SLOT + r].astype(jnp.float32)
        residual[place] -= tile
    for place in places.values():
        f = jnp.minimum(place, face_dev - 1)
        out[f] = updated(residual[f], blocks[f], traces[f])


def exchange(routes, swap, even):
    sibling, even_chips, odd_chips = routes
    from_even = lax.ppermute(even, "elem", even_chips)
    from_sib = lax.ppermute(swap, "elem", sibling)
    odd = jnp.concatenate([even[:SLOT], from_sib[SLOT:]])
    return from_sib, from_even, lax.ppermute(odd, "elem", odd_chips)


def per_device(devices, elem_mats, face_blocks, rhs, elem_faces, orient, counts):
    elem_cap, dof, _ = elem_mats.shape
    face_dev, functionals, trace_len = rhs.shape
    live = elem_cap - elem_cap // 4
    far = 4 * SLOT
    routes = swap_routes(devices)

    def in_hbm(array):
        return pltpu.with_memory_space_constraint(array, pltpu.HBM)

    def in_vmem(array):
        return pltpu.with_memory_space_constraint(array, pltpu.VMEM)

    faces = in_hbm(elem_faces.T)
    tables = jnp.asarray(lane_tables(trace_len))
    vmem = pl.BlockSpec(memory_space=pltpu.VMEM)
    smem = pl.BlockSpec(memory_space=pltpu.SMEM)
    hbm = pl.BlockSpec(memory_space=pltpu.HBM)

    def tiles(count, kind, width=LANES):
        return jax.ShapeDtypeStruct((count, functionals, width), kind)

    def integers(*shape):
        return jax.ShapeDtypeStruct(shape, jnp.int32)

    params = pltpu.CompilerParams(vmem_limit_bytes=4 << 20)
    counts_smem = pltpu.SMEM(counts.shape, jnp.int32)
    swap, even, slots = pl.pallas_call(
        functools.partial(first_kernel, elem_cap, devices),
        out_shape=(
            tiles(2 * SLOT, jnp.bfloat16),
            tiles(2 * SLOT, jnp.bfloat16),
            integers(far, LANES),
        ),
        in_specs=[hbm] * 4,
        out_specs=(vmem,) * 3,
        scratch_shapes=[
            pltpu.VMEM(faces.shape, jnp.int32),
            counts_smem,
            pltpu.VMEM(rhs.shape, rhs.dtype),
            pltpu.VMEM(face_blocks.shape, face_blocks.dtype),
            pltpu.SemaphoreType.DMA((4,)),
        ],
        compiler_params=params,
        cost_estimate=pl.CostEstimate(
            flops=10**11, bytes_accessed=10**8, transcendentals=0
        ),
        name="first_sweep",
    )(faces, in_hbm(counts), in_hbm(rhs), in_hbm(face_blocks))
    def passed_on(from_even, after):
        relay = pl.pallas_call(
            relay_kernel,
            out_shape=tiles(SLOT, jnp.bfloat16),
            in_specs=[vmem, pl.BlockSpec(memory_space=pl.ANY)],
            out_specs=vmem,
            compiler_params=params,
            name="relay",
        )(from_even, after)
        return lax.ppermute(relay, "elem", routes[0])

    from_sib, from_even, from_odd = exchange(routes, swap, even)
    all_terms = pltpu.VMEM((live + 1, functionals, 6 * LANES), jnp.float32)
    traces, rounded = pl.pallas_call(
        traces_kernel,
        out_shape=(tiles(face_dev, jnp.float32), tiles(face_dev, jnp.bfloat16)),
        in_specs=[vmem] * 2,
        out_specs=(vmem,) * 2,
        compiler_params=params,
        name="all_traces",
    )(rhs, face_blocks)
    rows, sums, remote, index_in = pl.pallas_call(
        functools.partial(rows_kernel, elem_cap),
        out_shape=(
            tiles(live, jnp.bfloat16, 6 * LANES),
            integers(6, LANES),
            integers(far, LANES),
            integers(far, LANES),
        ),
        in_specs=[vmem] * 6,
        out_specs=(vmem,) * 4,
        scratch_shapes=[pltpu.VMEM((face_dev + 1 + SLOT, functionals, LANES), jnp.bfloat16)],
        compiler_params=params,
        name="home_rows",
    )(elem_faces.T, orient.T, counts, tables, rounded, from_sib)
    terms = pl.pallas_call(
        home_kernel,
        out_shape=all_terms,
        in_specs=[vmem] * 2,
        out_specs=vmem,
        compiler_params=params,
        cost_estimate=pl.CostEstimate(
            flops=2 * live * functionals * dof * dof,
            bytes_accessed=2 * live * dof * dof,
            transcendentals=0,
        ),
        name="home_terms",
    )(rows, in_vmem(elem_mats))
    relayed = passed_on(from_even, sums)
    terms = pl.pallas_call(
        even_kernel,
        out_shape=all_terms,
        in_specs=[vmem] * 5,
        out_specs=vmem,
        input_output_aliases={4: 0},
        compiler_params=params,
        name="even_terms",
    )(remote, index_in, relayed, in_vmem(elem_mats), in_vmem(terms))
    swap, even, terms = pl.pallas_call(
        remote_kernel,
        out_shape=(tiles(2 * SLOT, jnp.bfloat16), tiles(2 * SLOT, jnp.bfloat16), all_terms),
        in_specs=[vmem] * 7,
        out_specs=(vmem,) * 3,
        input_output_aliases={6: 2},
        compiler_params=params,
        name="remote_terms",
    )(
        remote,
        index_in,
        tables,
        from_even,
        from_odd,
        in_vmem(elem_mats),
        in_vmem(terms),
    )
    from_sib, from_even, from_odd = exchange(routes, swap, even)
    base = pl.pallas_call(
        scatter_kernel,
        out_shape=tiles(face_dev + 1, jnp.float32),
        in_specs=[vmem] * 4,
        out_specs=vmem,
        compiler_params=params,
        name="home_sum",
    )(sums, tables, terms, rhs)
    relayed = passed_on(from_even, base)
    residual, early = pl.pallas_call(
        early_kernel,
        out_shape=(
            tiles(face_dev + 1, jnp.float32),
            jax.ShapeDtypeStruct(rhs.shape, jnp.float32),
        ),
        in_specs=[vmem] * 7,
        out_specs=(vmem,) * 2,
        compiler_params=params,
        name="early_update",
    )(slots, base, from_sib, from_even, relayed, face_blocks, traces)
    return pl.pallas_call(
        last_kernel,
        out_shape=jax.ShapeDtypeStruct(rhs.shape, jnp.float32),
        in_specs=[vmem] * 6,
        out_specs=vmem,
        scratch_shapes=[pltpu.VMEM((face_dev + 1, functionals, LANES), jnp.float32)],
        compiler_params=params,
        name="last_update",
    )(slots, residual, early, from_odd, face_blocks, traces)


def solution(mesh):
    in_specs = (P("elem", None, None), P("elem", None, None), P("elem", None, None), P(), P(), P())
    out_specs = P("elem", None, None)
    return jax.shard_map(
        functools.partial(per_device, mesh.shape["elem"]),
        mesh=mesh,
        in_specs=in_specs,
        out_specs=out_specs,
        check_vma=False,
    )
```

```python
import functools

import jax
import jax.numpy as jnp
import numpy as np
from jax import lax
from jax.experimental import pallas as pl
from jax.experimental.pallas import tpu as pltpu
from jax.sharding import PartitionSpec as P

COMP = 5
EDGE = 5
SLOT = 4
LANES = 128
SIB, EVEN, ODD, CROSS = range(4)


def orient_tables(edge_nodes, components):
    node_ids = np.arange(edge_nodes * edge_nodes)
    row_pos = node_ids // edge_nodes
    col_pos = node_ids % edge_nodes
    table_rows = []
    for orient_code in range(8):
        if orient_code & 4:
            first_pos, second_pos = (col_pos, row_pos)
        else:
            first_pos, second_pos = (row_pos, col_pos)
        if orient_code & 1:
            first_pos = edge_nodes - 1 - first_pos
        if orient_code & 2:
            second_pos = edge_nodes - 1 - second_pos
        moved_node = first_pos * edge_nodes + second_pos
        table_rows.append(
            np.concatenate(
                [
                    part_index * edge_nodes * edge_nodes + moved_node
                    for part_index in range(components)
                ]
            )
        )
    forward = np.stack(table_rows).astype(np.int32)
    backward = np.argsort(forward, axis=1).astype(np.int32)
    return (forward, backward)


def window_rows(trace_len):
    dof = 6 * trace_len
    for height in range(trace_len, dof):
        last = dof - height
        starts = [min(trace_len * k // 16 * 16, last) for k in range(6)]
        if last % 16 == 0 and all(
            start + height >= trace_len * (k + 1) for k, start in enumerate(starts)
        ):
            return height, last
    return dof, 0


def lane_tables(trace_len):
    forward, backward = orient_tables(EDGE, COMP)
    gap = LANES - trace_len
    spare = np.arange(trace_len, LANES)
    lanes = np.arange(LANES)
    _, last = window_rows(trace_len)
    into = np.zeros((6 * 8, LANES), np.int32)
    window = np.zeros((6 * 8, LANES), np.int32)
    outof = np.zeros((6 * 8, LANES), np.int32)
    for k in range(6):
        start = min(trace_len * k // 16 * 16, last)
        for code in range(8):
            full = np.concatenate([forward[code], spare])
            into[k * 8 + code] = full[(lanes + gap * k) % LANES]
            window[k * 8 + code] = full[(lanes - (trace_len * k - start)) % LANES]
            full = np.concatenate([backward[code], spare])
            outof[k * 8 + code] = (full - gap * k) % LANES
    return np.stack([into, window, outof])


def swap_routes(devices):
    routes = [[(i, i ^ 1) for i in range(devices)]]
    for shift in (0, 2):
        route = []
        for i in range(devices):
            other = ((i - shift) ^ 3) + shift
            route.append((i, other if i >= shift and other < devices else i ^ 1))
        routes.append(route)
    return routes


def partners(me):
    core = me & 1
    odd_chip = (me >> 1) & 1
    return (
        me ^ 1,
        me + 2 - 4 * odd_chip,
        me - 2 + 4 * odd_chip,
        me - 1 + 2 * core,
    )


def crossing_bucket(from_even, from_odd):
    me = lax.axis_index("elem")
    by_even = jnp.broadcast_to(((me ^ (me >> 1)) & 1) == 1, from_even.shape[1:])
    return [jnp.where(by_even, from_even[r], from_odd[r]) for r in range(SLOT)]


def put_bucket(group, r, tile, swap, even):
    target, first = {SIB: (swap, 0), ODD: (swap, SLOT), CROSS: (even, 0), EVEN: (even, SLOT)}[group]
    target[first + r] = tile


def start_all(pairs, sems):
    copies = [
        pltpu.make_async_copy(src, dst, sems.at[i]) for i, (src, dst) in enumerate(pairs)
    ]
    for copy in copies:
        copy.start()
    return copies


def permuted(tile, index):
    index = jnp.broadcast_to(index, tile.shape)
    return jnp.take_along_axis(tile, index, axis=1, mode="promise_in_bounds")


def lanes_from(array, start):
    width = 2 * LANES
    block = jnp.clip(start // LANES, 0, array.shape[1] // LANES - 2)
    window = array[:, pl.ds(pl.multiple_of(block * LANES, LANES), width)]
    shift = block * LANES - start
    window = jnp.concatenate([window, window[:2]])
    return pltpu.roll(window, jnp.where(shift < 0, shift + width, shift), 1)[:, :LANES]


def sum_before(counts, elem, elem_cap):
    elem = jnp.broadcast_to(elem, counts.shape)
    total = counts
    step = 1
    while step < elem_cap:
        total = total + jnp.where(elem >= step, pltpu.roll(total, step, 1), 0.0)
        step *= 2
    return total - counts


def wanted_faces(me, elem_cap, devices, face_dev, faces, counts):
    window = lanes_from(faces, (me - 2) * elem_cap)
    lane = lax.broadcasted_iota(jnp.int32, (1, LANES), 1)
    span = sum((lane >= elem_cap * q).astype(jnp.int32) for q in range(1, 6))
    elem = lane - elem_cap * span
    limit = jnp.zeros_like(lane)
    for q in (0, 1, 3, 4):
        device = me + q - 2
        inside = (device >= 0) & (device < devices)
        count = jnp.where(inside, counts[jnp.clip(device, 0, devices - 1)], 0)
        limit = jnp.where(span == q, count, limit)
    local = [(window[k : k + 1] - me * face_dev) for k in range(6)]
    hits = [(x >= 0) & (x < face_dev) & (elem < limit) for x in local]
    ones = [hit.astype(jnp.float32) for hit in hits]
    column = sum(ones)
    rank = sum_before(jnp.broadcast_to(column, (8, LANES)), elem, elem_cap)[:1]
    found = [jnp.zeros((1, LANES), jnp.float32) for _ in range(SLOT)]
    for k in range(6):
        value = jnp.where(hits[k], local[k].astype(jnp.float32), 0.0)
        for r in range(SLOT):
            found[r] = found[r] + jnp.where(rank == r, value, 0.0)
        rank = rank + ones[k]
    slots = []
    for device in partners(me):
        inside = (device >= 0) & (device < devices)
        for r in range(SLOT):
            slot = jnp.sum(jnp.where(span == device - me + 2, found[r], 0.0)).astype(jnp.int32)
            slots.append(jnp.where(inside, slot, face_dev))
    return slots


def first_traces(rhs, block):
    value = jnp.dot(rhs, block, preferred_element_type=jnp.float32)
    spare = jnp.zeros((value.shape[0], LANES - value.shape[1]), jnp.float32)
    return jnp.concatenate([value, spare], axis=1)


def first_kernel(
    elem_cap,
    devices,
    faces_hbm,
    counts_hbm,
    rhs_hbm,
    blocks_hbm,
    swap,
    even,
    slots,
    faces,
    counts,
    rhs,
    blocks,
    sems,
):
    me = lax.axis_index("elem")
    face_dev = rhs.shape[0]
    copies = start_all(
        [(faces_hbm, faces), (counts_hbm, counts), (rhs_hbm, rhs), (blocks_hbm, blocks)], sems
    )
    copies[0].wait()
    copies[1].wait()
    picked = wanted_faces(me, elem_cap, devices, face_dev, faces, counts)
    for i, slot in enumerate(picked):
        slots[i : i + 1, :] = jnp.full((1, LANES), slot)
    copies[2].wait()
    copies[3].wait()
    for group in range(4):
        for r in range(SLOT):
            f = jnp.minimum(picked[group * SLOT + r], face_dev - 1)
            tile = first_traces(rhs[f], blocks[f]).astype(jnp.bfloat16)
            put_bucket(group, r, tile, swap, even)


def own_lists(me, elem_cap, face_dev, faces, orient, counts):
    window = lanes_from(faces, me * elem_cap)
    codes = lanes_from(orient, me * elem_cap)
    lane = lax.broadcasted_iota(jnp.int32, (1, LANES), 1)
    every = lax.broadcasted_iota(jnp.int32, (1, counts.shape[0]), 1)
    count = jnp.sum(jnp.where(every == me, counts[...].reshape(every.shape), 0).astype(jnp.float32))
    used = lane.astype(jnp.float32) < count
    rel = [window[k : k + 1] - (me - 2) * face_dev for k in range(6)]
    owner = [sum((x >= face_dev * j).astype(jnp.int32) for j in range(1, 5)) for x in rel]
    owner = [jnp.where(used, x, 2) for x in owner]
    others = [0, 1, 3, 4]
    column = [sum((x == j).astype(jnp.float32) for x in owner) for j in others]
    column = jnp.concatenate(column + [jnp.zeros((4, LANES), jnp.float32)])
    ranks = sum_before(column, lane, elem_cap).astype(jnp.int32)
    heads = []
    for i, j in enumerate(others):
        base = sum(
            jnp.where(device == me + j - 2, group * SLOT, 0)
            for group, device in enumerate(partners(me))
        )
        heads.append(ranks[i : i + 1] + base)
    gather, home, slots, picks = [], [], [], []
    for k in range(6):
        slot = jnp.full_like(lane, 4 * SLOT)
        for i, j in enumerate(others):
            hit = owner[k] == j
            slot = jnp.where(hit, heads[i], slot)
            heads[i] = heads[i] + hit.astype(jnp.int32)
        place = jnp.where(used & (owner[k] == 2), rel[k] - 2 * face_dev, face_dev)
        gather.append(jnp.where(slot < SLOT, face_dev + 1 + slot, place))
        home.append(place)
        slots.append(slot)
        picks.append(codes[k : k + 1] + 8 * k)
    return gather, home, slots, picks


def rows_kernel(
    elem_cap,
    faces,
    orient,
    counts,
    tables,
    rhs,
    blocks,
    from_sib,
    traces,
    rows,
    sums,
    remote,
    index_in,
    table,
):
    me = lax.axis_index("elem")
    face_dev, functionals, _ = rhs.shape
    live = rows.shape[0]
    trace_len = COMP * EDGE * EDGE
    gap = LANES - trace_len
    for f in range(face_dev):
        value = first_traces(rhs[f], blocks[f])
        traces[f] = value
        table[f] = value.astype(jnp.bfloat16)
    table[face_dev] = jnp.zeros((functionals, LANES), jnp.bfloat16)
    table[face_dev + 1 :] = from_sib[:SLOT]
    gather, home, slots, picks = own_lists(me, elem_cap, face_dev, faces, orient, counts)
    packed = [gather[k] * 64 + picks[k] for k in range(6)]
    for k in range(6):
        sums[k : k + 1, :] = home[k] * 64 + picks[k]
    lane = lax.broadcasted_iota(jnp.int32, (functionals, LANES), 1)
    for e in range(live):
        parts = []
        for k in range(6):
            code = packed[k][0, e]
            tile = table[code >> 6].astype(jnp.float32)
            parts.append(permuted(tile, tables[0, pl.ds(code & 63, 1), :]))
        for k in range(6):
            later = parts[k + 1] if k < 5 else jnp.zeros_like(parts[k])
            merged = jnp.where(lane < trace_len - gap * k, parts[k], later)
            rows[e, :, k * LANES : (k + 1) * LANES] = merged.astype(jnp.bfloat16)
    elem = lax.broadcasted_iota(jnp.int32, (1, LANES), 1)
    for t in range(4 * SLOT):
        entry = jnp.zeros((1, LANES), jnp.float32)
        for k in range(6):
            code = ((elem - live) * 8 + k) * 64 + picks[k]
            entry = entry + jnp.where(slots[k] == t, code.astype(jnp.float32), 0.0)
        code = jnp.sum(entry).astype(jnp.int32) + live * 512
        remote[t : t + 1, :] = jnp.full((1, LANES), code)
        index_in[t : t + 1, :] = tables[1, pl.ds(code & 63, 1), :]


def home_kernel(rows, mats, terms):
    live = rows.shape[0]
    dof = mats.shape[1]
    for e in range(live):
        terms[e, :, :dof] = jnp.dot(rows[e, :, :dof], mats[e], preferred_element_type=jnp.float32)
    terms[live] = jnp.zeros(terms.shape[1:], jnp.float32)


def unpacked(packs, t):
    packed = packs[t, 0]
    return packed >> 9, (packed >> 6) & 7, packed & 63


def add_remote(group, arrived, first, packs, index_in, mats, terms):
    live = terms.shape[0] - 1
    trace_len = mats.shape[1] // 6
    gap = LANES - trace_len
    height, last = window_rows(trace_len)
    lane = lax.broadcasted_iota(jnp.int32, arrived[first].shape, 1)
    for r in range(SLOT):
        t = group * SLOT + r
        e, k, _ = unpacked(packs, t)
        start = jnp.minimum((trace_len * k) >> 4 << 4, last)
        shift = trace_len * k - start
        tile = permuted(arrived[first + r].astype(jnp.float32), index_in[t : t + 1, :])
        zero = jnp.zeros_like(tile)
        wide = jnp.concatenate(
            [
                jnp.where((lane >= shift) & (lane < shift + trace_len), tile, zero),
                jnp.where(lane < shift - gap, tile, zero),
            ],
            axis=1,
        ).astype(jnp.bfloat16)
        window = mats[jnp.minimum(e, live - 1), pl.ds(pl.multiple_of(start, 16), height), :]
        terms[e, :, : 6 * trace_len] += jnp.dot(
            wide[:, :height], window, preferred_element_type=jnp.float32
        )


def relay_kernel(from_even, _, out):
    out[...] = from_even[SLOT:]


def even_kernel(remote, index_in, relayed, mats, _, terms):
    add_remote(EVEN, relayed, 0, remote[...], index_in, mats, terms)


def remote_kernel(
    remote, index_in, tables, from_even, from_odd, mats, _, swap, even, terms
):
    trace_len = mats.shape[1] // 6
    gap = LANES - trace_len
    packs = remote[...]
    add_remote(CROSS, crossing_bucket(from_even, from_odd), 0, packs, index_in, mats, terms)
    add_remote(ODD, from_odd, SLOT, packs, index_in, mats, terms)
    lane = lax.broadcasted_iota(jnp.int32, from_odd.shape[1:], 1)
    for group in range(4):
        for r in range(SLOT):
            e, k, pick = unpacked(packs, group * SLOT + r)
            tile = terms[e, :, pl.ds(pl.multiple_of(k * LANES, LANES), LANES)]
            ahead = jnp.maximum(k - 1, 0)
            left = terms[e, :, pl.ds(pl.multiple_of(ahead * LANES, LANES), LANES)]
            tile = jnp.where(lane >= LANES - gap * k, left, tile)
            tile = permuted(tile, tables[2, pl.ds(pick, 1), :]).astype(jnp.bfloat16)
            put_bucket(group, r, tile, swap, even)


def scatter_kernel(sums, tables, terms, rhs, base):
    face_dev, functionals, trace_len = rhs.shape
    live = terms.shape[0] - 1
    gap = LANES - trace_len
    lane = lax.broadcasted_iota(jnp.int32, (functionals, LANES), 1)
    base[:face_dev, :, :trace_len] = rhs[...].astype(jnp.float32)
    base[face_dev] = jnp.zeros((functionals, LANES), jnp.float32)
    codes = sums[...]
    for e in range(live):
        for k in range(6):
            tile = terms[e, :, k * LANES : (k + 1) * LANES]
            if k:
                left = terms[e, :, (k - 1) * LANES : k * LANES]
                tile = jnp.where(lane >= LANES - gap * k, left, tile)
            code = codes[k, e]
            tile = permuted(tile, tables[2, pl.ds(code & 63, 1), :])
            place = code >> 6
            base[place] -= tile.astype(jnp.bfloat16).astype(jnp.float32)


def updated(residual, block, trace):
    trace_len = block.shape[0]
    update = jnp.dot(
        residual[:, :trace_len].astype(jnp.bfloat16), block, preferred_element_type=jnp.float32
    )
    return trace[:, :trace_len] + update


def crossing_part(arrived, by_even):
    me = lax.axis_index("elem")
    here = (((me ^ (me >> 1)) & 1) == 1) == by_even
    here = jnp.broadcast_to(here, arrived.shape[1:])
    return [jnp.where(here, arrived[r].astype(jnp.float32), 0.0) for r in range(SLOT)]


def early_kernel(slots, base, from_sib, from_even, relayed, blocks, traces, residual, early):
    face_dev = early.shape[0]
    residual[...] = base[...]
    crossing = crossing_part(from_even, True)
    places = slots[...]
    for r in range(SLOT):
        arrived = {SIB: from_sib[r], EVEN: relayed[r], CROSS: crossing[r]}
        for group, tile in arrived.items():
            place = places[group * SLOT + r, 0]
            residual[place] -= tile.astype(jnp.float32)
    for f in range(face_dev):
        early[f] = updated(residual[f], blocks[f], traces[f])


def last_kernel(slots, before, early, from_odd, blocks, traces, out, residual):
    face_dev = out.shape[0]
    residual[...] = before[...]
    out[...] = early[...]
    crossing = crossing_part(from_odd, False)
    codes = slots[...]
    places = {(g, r): codes[g * SLOT + r, 0] for g in (ODD, CROSS) for r in range(SLOT)}
    for (group, r), place in places.items():
        tile = crossing[r] if group == CROSS else from_odd[SLOT + r].astype(jnp.float32)
        residual[place] -= tile
    for place in places.values():
        f = jnp.minimum(place, face_dev - 1)
        out[f] = updated(residual[f], blocks[f], traces[f])


def exchange(routes, swap, even):
    sibling, even_chips, odd_chips = routes
    from_even = lax.ppermute(even, "elem", even_chips)
    from_sib = lax.ppermute(swap, "elem", sibling)
    odd = jnp.concatenate([even[:SLOT], from_sib[SLOT:]])
    return from_sib, from_even, lax.ppermute(odd, "elem", odd_chips)


def per_device(devices, elem_mats, face_blocks, rhs, elem_faces, orient, counts):
    elem_cap, dof, _ = elem_mats.shape
    face_dev, functionals, trace_len = rhs.shape
    live = elem_cap - elem_cap // 4
    far = 4 * SLOT
    routes = swap_routes(devices)

    def in_hbm(array):
        return pltpu.with_memory_space_constraint(array, pltpu.HBM)

    def in_vmem(array):
        return pltpu.with_memory_space_constraint(array, pltpu.VMEM)

    faces = in_hbm(elem_faces.T)
    tables = jnp.asarray(lane_tables(trace_len))
    vmem = pl.BlockSpec(memory_space=pltpu.VMEM)
    smem = pl.BlockSpec(memory_space=pltpu.SMEM)
    hbm = pl.BlockSpec(memory_space=pltpu.HBM)

    def tiles(count, kind, width=LANES):
        return jax.ShapeDtypeStruct((count, functionals, width), kind)

    def integers(*shape):
        return jax.ShapeDtypeStruct(shape, jnp.int32)

    params = pltpu.CompilerParams(vmem_limit_bytes=4 << 20)
    counts_smem = pltpu.SMEM(counts.shape, jnp.int32)
    swap, even, slots = pl.pallas_call(
        functools.partial(first_kernel, elem_cap, devices),
        out_shape=(
            tiles(2 * SLOT, jnp.bfloat16),
            tiles(2 * SLOT, jnp.bfloat16),
            integers(far, LANES),
        ),
        in_specs=[hbm] * 4,
        out_specs=(vmem,) * 3,
        scratch_shapes=[
            pltpu.VMEM(faces.shape, jnp.int32),
            counts_smem,
            pltpu.VMEM(rhs.shape, rhs.dtype),
            pltpu.VMEM(face_blocks.shape, face_blocks.dtype),
            pltpu.SemaphoreType.DMA((4,)),
        ],
        compiler_params=params,
        cost_estimate=pl.CostEstimate(
            flops=10**11, bytes_accessed=10**8, transcendentals=0
        ),
        name="first_sweep",
    )(faces, in_hbm(counts), in_hbm(rhs), in_hbm(face_blocks))
    def passed_on(from_even, after):
        relay = pl.pallas_call(
            relay_kernel,
            out_shape=tiles(SLOT, jnp.bfloat16),
            in_specs=[vmem, pl.BlockSpec(memory_space=pl.ANY)],
            out_specs=vmem,
            compiler_params=params,
            name="relay",
        )(from_even, after)
        return lax.ppermute(relay, "elem", routes[0])

    from_sib, from_even, from_odd = exchange(routes, swap, even)
    all_terms = pltpu.VMEM((live + 1, functionals, 6 * LANES), jnp.float32)
    traces, rows, sums, remote, index_in = pl.pallas_call(
        functools.partial(rows_kernel, elem_cap),
        out_shape=(
            tiles(face_dev, jnp.float32),
            tiles(live, jnp.bfloat16, 6 * LANES),
            integers(6, LANES),
            integers(far, LANES),
            integers(far, LANES),
        ),
        in_specs=[vmem] * 7,
        out_specs=(vmem,) * 5,
        scratch_shapes=[pltpu.VMEM((face_dev + 1 + SLOT, functionals, LANES), jnp.bfloat16)],
        compiler_params=params,
        name="home_rows",
    )(elem_faces.T, orient.T, counts, tables, rhs, face_blocks, from_sib)
    terms = pl.pallas_call(
        home_kernel,
        out_shape=all_terms,
        in_specs=[vmem] * 2,
        out_specs=vmem,
        compiler_params=params,
        cost_estimate=pl.CostEstimate(
            flops=2 * live * functionals * dof * dof,
            bytes_accessed=2 * live * dof * dof,
            transcendentals=0,
        ),
        name="home_terms",
    )(rows, in_vmem(elem_mats))
    relayed = passed_on(from_even, sums)
    terms = pl.pallas_call(
        even_kernel,
        out_shape=all_terms,
        in_specs=[vmem] * 5,
        out_specs=vmem,
        input_output_aliases={4: 0},
        compiler_params=params,
        name="even_terms",
    )(remote, index_in, relayed, in_vmem(elem_mats), in_vmem(terms))
    swap, even, terms = pl.pallas_call(
        remote_kernel,
        out_shape=(tiles(2 * SLOT, jnp.bfloat16), tiles(2 * SLOT, jnp.bfloat16), all_terms),
        in_specs=[vmem] * 7,
        out_specs=(vmem,) * 3,
        input_output_aliases={6: 2},
        compiler_params=params,
        name="remote_terms",
    )(
        remote,
        index_in,
        tables,
        from_even,
        from_odd,
        in_vmem(elem_mats),
        in_vmem(terms),
    )
    from_sib, from_even, from_odd = exchange(routes, swap, even)
    base = pl.pallas_call(
        scatter_kernel,
        out_shape=tiles(face_dev + 1, jnp.float32),
        in_specs=[vmem] * 4,
        out_specs=vmem,
        compiler_params=params,
        name="home_sum",
    )(sums, tables, terms, rhs)
    relayed = passed_on(from_even, base)
    residual, early = pl.pallas_call(
        early_kernel,
        out_shape=(
            tiles(face_dev + 1, jnp.float32),
            jax.ShapeDtypeStruct(rhs.shape, jnp.float32),
        ),
        in_specs=[vmem] * 7,
        out_specs=(vmem,) * 2,
        compiler_params=params,
        name="early_update",
    )(slots, base, from_sib, from_even, relayed, face_blocks, traces)
    return pl.pallas_call(
        last_kernel,
        out_shape=jax.ShapeDtypeStruct(rhs.shape, jnp.float32),
        in_specs=[vmem] * 6,
        out_specs=vmem,
        scratch_shapes=[pltpu.VMEM((face_dev + 1, functionals, LANES), jnp.float32)],
        compiler_params=params,
        name="last_update",
    )(slots, residual, early, from_odd, face_blocks, traces)


def solution(mesh):
    in_specs = (P("elem", None, None), P("elem", None, None), P("elem", None, None), P(), P(), P())
    out_specs = P("elem", None, None)
    return jax.shard_map(
        functools.partial(per_device, mesh.shape["elem"]),
        mesh=mesh,
        in_specs=in_specs,
        out_specs=out_specs,
        check_vma=False,
    )
```
